128 devices in a mesh: aux: 4 (over y_lo, core), blk: 32 (over y_hi, z, x).
Axes of the slice: x: 4, y: 4 (y_hi: 2, y_lo: 2; y = y_hi * 2 + y_lo), z: 4, core: 2. Of those that a mesh axis runs over, the one named last changes fastest.
Arguments:
- b_factors: bfloat16 [8192, 64, 128], P('blk', 'aux'), may hold values from -0.3125 to 0.3125
Outputs:
- exchange: float32 [8192, 8192], P('blk', 'aux')
The draws below stay inside these ranges and needn't reach their ends.
All inputs are finite; a program needn't handle non-finite values.
Results may differ from the reference program's by a relative error of at most 0.0003.
Values may be sent and summed in bfloat16 or wider, within the bound.
No kernel may reach another device: no remote copies, remote signals or barrier semaphores. Data moves between devices by JAX's collectives and lax.ppermute only.
A program may use at most 128 MiB of HBM per device.

```python
import jax
import jax.numpy as jnp

NOCC = 128
NBF = 8192
AUX = 64


def block_levels(own_key, dims, pieces, smallest, top_value):
    def one(dim, blocks):
        heights = jax.random.uniform(jax.random.fold_in(jax.random.fold_in(own_key, 6), dim), (blocks,), jnp.float32, smallest / len(pieces), top_value / len(pieces))
        return jnp.repeat(jnp.exp(heights), dims[dim] // blocks).reshape((-1,) + (1,) * (len(dims) - dim - 1))

    gain = one(*pieces[0])
    for cut in pieces[1:]:
        gain = gain * one(*cut)
    return gain


def noise(rng, dims, width, limit, split=(), kind=jnp.bfloat16):
    values = jax.random.normal(rng, dims, jnp.float32) * width
    if len(split) > 0:
        values = block_levels(rng, dims, split, -0.22, 0.18) * values
    return jnp.clip(values, min=-limit, max=limit).astype(kind)


def setup_inputs(seed: int = 0) -> dict:
    streams_of = jax.random.split(jax.random.key(seed), 2)
    return {
        "b_factors": noise(streams_of[0], (NBF, AUX, NOCC), 0.022, 0.3125, ((0, 32), (1, 4))),
    }


def reference(b_factors):
    flat = b_factors.reshape(b_factors.shape[0], -1)
    return jnp.dot(flat, flat.T, preferred_element_type=jnp.float32)
```

```python
import functools
import math

import jax
import jax.numpy as jnp
from jax import lax
from jax.experimental import pallas as pl
from jax.experimental.pallas import tpu as pltpu
from jax.sharding import PartitionSpec as P

ORDER = 32
TOP = 2.0**3.9
FLOOR = 2.0**-3.9
VMEM = 48 << 20

DEVICES = [
    (x, z, yh, yl, c)
    for yl in range(2)
    for c in range(2)
    for yh in range(2)
    for z in range(4)
    for x in range(4)
]


def move(value, where):
    index = {d: i for i, d in enumerate(DEVICES)}
    pairs = [(index[d], index[where(*d)]) for d in DEVICES]
    return lax.ppermute(value, ("aux", "blk"), pairs)


def to_own_layer(x, z, yh, yl, c):
    return x, z, c, yl, yh


def to_core(x, z, yh, yl, c):
    return x, z, yh, yl, 1 - c


def to_position(dx, dz, swap=False):
    def where(x, z, yh, yl, c):
        x, z = (x + dx) % 4, (z + dz) % 4
        return (x, z, yl, yh, c) if swap else (x, z, yh, yl, c)

    return where


def to_owner(m1, m2):
    def where(x, z, yh, yl, c):
        return x, z, c, yl ^ m1, yh ^ m2

    return where


MATCHINGS = ((0, 0), (0, 1), (1, 0), (1, 1))


def product(a, b):
    return lax.dot_general(a, b, (((1,), (1,)), ((), ())), preferred_element_type=jnp.float32)


def encode(value, bound):
    v = jnp.abs(value) * (TOP / bound) + FLOOR
    for _ in range(int(math.log2(ORDER))):
        v = v * v
    return jnp.where(value < 0, -v, v).astype(jnp.bfloat16)


def decode(code, bound):
    y = code.astype(jnp.float32)
    v = jnp.exp(jnp.log(jnp.abs(y)) * (1.0 / ORDER)) - FLOOR
    return jnp.where(y < 0, -v, v) * (bound * (1.0 / TOP))


def tiles_kernel(classes, n_in, place, *refs):
    ins, outs, acc = refs[:n_in], refs[n_in : n_in + 4], refs[n_in + 4]
    yh, yl, c = place[0], place[1], place[2]
    half = acc.shape[1] // 2
    width = acc.shape[2]
    count = len(classes)
    row = lax.broadcasted_iota(jnp.int32, (16, width), 0)
    bounds = jnp.zeros((16, width), jnp.float32)
    for k, (rows, own, other) in enumerate(classes):
        for slot, columns in ((c, own), (1 - c, other)):
            r0 = 0
            for r in rows:
                c0 = 0
                for q in columns:
                    h, w = ins[r].shape[0], ins[q].shape[0]
                    acc[slot, r0 : r0 + h, c0 : c0 + w] = product(ins[r][...], ins[q][...])
                    c0 += w
                r0 += h
        top = jnp.maximum(jnp.max(jnp.abs(acc[...])), 1e-30) * 1.008
        coded = jnp.full((16, width), top, jnp.float32).astype(jnp.bfloat16).astype(jnp.float32)
        bounds = jnp.where(row == k, coded, bounds)
        bound = coded[0:1, :]
        for (m1, m2), out in zip(MATCHINGS, outs):
            part = acc[yl ^ m1, pl.ds(pl.multiple_of((yh ^ m2) * half, half), half), :]
            out[k * half : (k + 1) * half, :] = encode(part, bound)
    for out in outs:
        out[count * half :, :] = bounds.astype(jnp.bfloat16)


def partial_tiles(place, blocks, classes, rows):
    names, arrays, ids = list(blocks), [], {}
    for name in names:
        ids[name] = tuple(range(len(arrays), len(arrays) + len(blocks[name])))
        arrays += blocks[name]
    listed = tuple((ids[r], ids[o], ids[t]) for r, o, t in classes)
    out = jax.ShapeDtypeStruct((len(classes) * (rows // 2) + 16, rows), jnp.bfloat16)
    flops = len(classes) * 4 * rows * rows * arrays[0].shape[1]
    return pl.pallas_call(
        functools.partial(tiles_kernel, listed, len(arrays)),
        out_shape=[out] * 4,
        in_specs=[pl.BlockSpec(memory_space=pltpu.SMEM)]
        + [pl.BlockSpec(memory_space=pltpu.VMEM)] * len(arrays),
        out_specs=[pl.BlockSpec(memory_space=pltpu.VMEM)] * 4,
        scratch_shapes=[pltpu.VMEM((2, rows, rows), jnp.float32)],
        compiler_params=pltpu.CompilerParams(vmem_limit_bytes=VMEM),
        cost_estimate=pl.CostEstimate(flops=flops, bytes_accessed=1 << 23, transcendentals=0),
    )(place, *arrays)


def sum_kernel(groups, *refs):
    ins, outs = refs[:4], refs[4:]
    half, width = outs[0].shape[1], outs[0].shape[2]
    count = (ins[0].shape[0] - 16) // half
    for k in range(count):
        total = None
        for r in ins:
            bound = r[count * half :, :].astype(jnp.float32)[k : k + 1, :]
            term = decode(r[k * half : (k + 1) * half, :], bound)
            total = term if total is None else total + term
        for out, members in zip(outs, groups):
            for i, member in enumerate(members):
                if member == k:
                    out[i, :, :] = total


def summed(coded, groups, rows):
    return pl.pallas_call(
        functools.partial(sum_kernel, groups),
        out_shape=[jax.ShapeDtypeStruct((len(g), rows // 2, rows), jnp.float32) for g in groups],
        in_specs=[pl.BlockSpec(memory_space=pltpu.VMEM)] * 4,
        out_specs=[pl.BlockSpec(memory_space=pltpu.VMEM)] * len(groups),
        compiler_params=pltpu.CompilerParams(vmem_limit_bytes=VMEM),
        cost_estimate=pl.CostEstimate(flops=1 << 24, bytes_accessed=1 << 22, transcendentals=1 << 21),
    )(*coded)


def place_kernel(tiles, n, place, *refs):
    own, other, out = refs[:n], refs[n : 2 * n], refs[2 * n]
    c, z, x = place[2], place[3], place[4]
    rows = out.shape[0]
    half = rows // 2
    for array, i, (dx, dz), turned in tiles:
        zz = (z + dz) % 4
        xx = (x + dx) % 4

        @pl.when(zz // 2 == c)
        def _():
            start = pl.multiple_of(((zz % 2) * 4 + xx) * rows, rows)
            first = pl.multiple_of(c * half, half)
            second = pl.multiple_of((1 - c) * half, half)
            if turned:
                out[:, pl.ds(pl.multiple_of(start + first, half), half)] = own[array][i, :, :].T
                out[:, pl.ds(pl.multiple_of(start + second, half), half)] = other[array][i, :, :].T
            else:
                out[pl.ds(first, half), pl.ds(start, rows)] = own[array][i, :, :]
                out[pl.ds(second, half), pl.ds(start, rows)] = other[array][i, :, :]


def placed(place, own, other, tiles, rows):
    n = len(own)
    return pl.pallas_call(
        functools.partial(place_kernel, tiles, n),
        out_shape=jax.ShapeDtypeStruct((rows, 8 * rows), jnp.float32),
        in_specs=[pl.BlockSpec(memory_space=pltpu.SMEM)]
        + [pl.BlockSpec(memory_space=pltpu.VMEM)] * (2 * n),
        out_specs=pl.BlockSpec(memory_space=pltpu.VMEM),
        compiler_params=pltpu.CompilerParams(vmem_limit_bytes=VMEM),
        cost_estimate=pl.CostEstimate(flops=0, bytes_accessed=6 << 20, transcendentals=0),
    )(place, *own, *other)


O, PX, MX, PZ, MZ, PE, ME = (0, 0), (1, 0), (3, 0), (0, 1), (0, 3), (1, 1), (3, 3)
EARLY = ((O, O), (O, PX), (O, PZ), (MX, PX), (MZ, PZ), (MZ, PX), (PZ, PX))
LATE = ((MX, PE), (MZ, PE), (ME, PE))
EARLY_SENDS = (
    (O, False, (0, 1, 2)),
    (MX, False, (3,)),
    (MZ, False, (4, 5)),
    (PZ, False, (6,)),
    (PX, True, (1, 5, 6)),
    (PZ, True, (2,)),
)
LATE_SENDS = (
    (MX, False, (0,)),
    (MZ, False, (1,)),
    (ME, False, (2,)),
    (PE, True, (0, 1)),
)


def minus(a, b):
    return (a[0] - b[0]) % 4, (a[1] - b[1]) % 4


def deliver(groups, sends):
    return [
        g if to == O else move(g, to_position(*to, swap=turned))
        for g, (to, turned, _) in zip(groups, sends)
    ]


def local(b_factors):
    rows = b_factors.shape[0]
    half = rows // 2
    flat = b_factors.reshape(rows, -1)
    aux, blk = lax.axis_index("aux"), lax.axis_index("blk")
    place = jnp.stack(
        [blk // 16, aux // 2, aux % 2, (blk // 4) % 4, blk % 4]
    ).astype(jnp.int32)

    own = {O: (move(flat, to_own_layer),)}
    base = own[O][0]
    for o in (PX, MX, PZ, MZ):
        own[o] = (move(base, to_position(-o[0], -o[1])),)
    other = {o: (move(own[o][0], to_core),) for o in (O, PX, PZ)}
    own[PE] = (
        move(own[PZ][0][:half], to_position(-1, 0)),
        move(own[PX][0][half:], to_position(0, -1)),
    )
    own[ME] = (
        move(own[MZ][0][:half], to_position(1, 0)),
        move(own[MX][0][half:], to_position(0, 1)),
    )
    other[PE] = tuple(move(v, to_core) for v in own[PE])

    own_parts, other_parts, tiles = [], [], []
    for classes, sends in ((EARLY, EARLY_SENDS), (LATE, LATE_SENDS)):
        needed = {r for r, _ in classes} | {q for _, q in classes}
        blocks = {("own", o): own[o] for o in own if o in needed}
        blocks |= {("other", q): other[q] for q in other if q in {b for _, b in classes}}
        coded = partial_tiles(
            place, blocks, [(("own", r), ("own", q), ("other", q)) for r, q in classes], rows
        )
        arrived = [move(v, to_owner(*m)) for v, m in zip(coded, MATCHINGS)]
        groups = summed(arrived, [members for _, _, members in sends], rows)
        parts = deliver(groups, sends)
        for (to, turned, members) in sends:
            for i, k in enumerate(members):
                r, q = classes[k]
                d = minus(r, q) if turned else minus(q, r)
                tiles.append((len(own_parts), i, d, turned))
            own_parts.append(parts.pop(0))
            other_parts.append(move(own_parts[-1], to_core))
    return placed(place, own_parts, other_parts, tuple(tiles), rows)


def solution(mesh):
    return jax.shard_map(
        local, mesh=mesh, in_specs=(P("blk", "aux", None),), out_specs=P("blk", "aux"), check_vma=False
    )
```

```python
import functools
import math

import jax
import jax.numpy as jnp
from jax import lax
from jax.experimental import pallas as pl
from jax.experimental.pallas import tpu as pltpu
from jax.sharding import PartitionSpec as P

ORDER = 32
TOP = 2.0**3.9
FLOOR = 2.0**-3.9
VMEM = 20 << 20

DEVICES = [
    (x, z, yh, yl, c)
    for yl in range(2)
    for c in range(2)
    for yh in range(2)
    for z in range(4)
    for x in range(4)
]


def move(value, where):
    index = {d: i for i, d in enumerate(DEVICES)}
    pairs = [(index[d], index[where(*d)]) for d in DEVICES]
    return lax.ppermute(value, ("aux", "blk"), pairs)


def to_own_layer(x, z, yh, yl, c):
    return x, z, c, yl, yh


def to_core(x, z, yh, yl, c):
    return x, z, yh, yl, 1 - c


def to_position(dx, dz, swap=False):
    def where(x, z, yh, yl, c):
        x, z = (x + dx) % 4, (z + dz) % 4
        return (x, z, yl, yh, c) if swap else (x, z, yh, yl, c)

    return where


def to_owner(m1):
    def where(x, z, yh, yl, c):
        return x, z, c, yl ^ m1, yh

    return where


def product(a, b):
    return lax.dot_general(a, b, (((1,), (1,)), ((), ())), preferred_element_type=jnp.float32)


def encode(value, bound):
    v = jnp.abs(value) * (TOP / bound) + FLOOR
    for _ in range(int(math.log2(ORDER))):
        v = v * v
    return jnp.where(value < 0, -v, v).astype(jnp.bfloat16)


def decode(code, bound):
    y = code.astype(jnp.float32)
    v = jnp.exp(jnp.log(jnp.abs(y)) * (1.0 / ORDER)) - FLOOR
    return jnp.where(y < 0, -v, v) * (bound * (1.0 / TOP))


def bound_of(top, width):
    rows = jnp.full((16, width), jnp.maximum(top, 1e-30) * 1.008, jnp.float32)
    return rows.astype(jnp.bfloat16).astype(jnp.float32)


def coded_shape(count, rows):
    return jax.ShapeDtypeStruct((count * rows + 16, rows), jnp.bfloat16)


def tile_of(ref, k):
    rows = ref.shape[1]
    bound = ref[ref.shape[0] - 16 :, :].astype(jnp.float32)[k : k + 1, :]
    return decode(ref[k * rows : (k + 1) * rows, :], bound)


def call(kernel, args, out_shape, scratch=(), any_from=None, flops=0, moved=0, transcendentals=0):
    whole = pl.BlockSpec(memory_space=pltpu.VMEM)
    specs = []
    for i, a in enumerate(args):
        if a.dtype == jnp.int32:
            specs.append(pl.BlockSpec(memory_space=pltpu.SMEM))
        else:
            specs.append(pl.BlockSpec(memory_space=pl.ANY) if any_from is not None and i >= any_from else whole)
    many = isinstance(out_shape, (list, tuple))
    return pl.pallas_call(
        kernel,
        out_shape=out_shape,
        in_specs=specs,
        out_specs=[whole] * len(out_shape) if many else whole,
        scratch_shapes=scratch,
        compiler_params=pltpu.CompilerParams(vmem_limit_bytes=VMEM),
        cost_estimate=pl.CostEstimate(flops=flops, bytes_accessed=moved, transcendentals=transcendentals),
    )(*args)


def tiles_kernel(classes, n_in, n_extra, place, *refs):
    ins = refs[:n_in]
    outs, (held, acc, sems) = refs[n_in + n_extra : n_in + n_extra + 2], refs[n_in + n_extra + 2 :]
    yl, c = place[1], place[2]
    rows = acc.shape[1]
    copies = [pltpu.make_async_copy(r, held.at[i], sems.at[i]) for i, r in enumerate(ins)]
    for copy in copies:
        copy.start()
    ready = set()
    row = lax.broadcasted_iota(jnp.int32, (16, rows), 0)
    bounds = jnp.zeros((16, rows), jnp.float32)
    for k, (r, own, other) in enumerate(classes):
        for i in (r, own, other):
            if i not in ready:
                copies[i].wait()
                ready.add(i)
        acc[c] = product(held[r], held[own])
        acc[1 - c] = product(held[r], held[other])
        coded = bound_of(jnp.max(jnp.abs(acc[...])), rows)
        bounds = jnp.where(row == k, coded, bounds)
        for m1, out in enumerate(outs):
            out[k * rows : (k + 1) * rows, :] = encode(acc[yl ^ m1], coded[0:1, :])
    for out in outs:
        out[len(classes) * rows :, :] = bounds.astype(jnp.bfloat16)


def partial_tiles(place, blocks, classes, rows, after=()):
    names = list(blocks)
    listed = tuple(tuple(names.index(n) for n in k) for k in classes)
    arrays = list(blocks.values())
    depth = arrays[0].shape[1]
    return call(
        functools.partial(tiles_kernel, listed, len(arrays), len(after)),
        [place, *arrays, *after],
        [coded_shape(len(classes), rows)] * 2,
        scratch=[
            pltpu.VMEM((len(arrays), rows, depth), jnp.bfloat16),
            pltpu.VMEM((2, rows, rows), jnp.float32),
            pltpu.SemaphoreType.DMA((len(arrays),)),
        ],
        any_from=1,
        flops=len(classes) * 4 * rows * rows * depth,
        moved=len(arrays) * rows * depth * 2,
    )


def sum_kernel(a, b, out):
    for k in range(out.shape[0]):
        out[k, :, :] = tile_of(a, k) + tile_of(b, k)


def group_kernel(groups, coded, a, b, *outs):
    rows = a.shape[1]
    row = lax.broadcasted_iota(jnp.int32, (16, rows), 0)
    bounds = [jnp.zeros((16, rows), jnp.float32) for _ in groups]
    for k in range(a.shape[0]):
        total = a[k, :, :] + b[k, :, :]
        bound = bound_of(jnp.max(jnp.abs(total)), rows)
        code = encode(total, bound[0:1, :]) if any(k in g and s for g, s in zip(groups, coded)) else None
        for j, (out, members) in enumerate(zip(outs, groups)):
            for i, member in enumerate(members):
                if member == k and coded[j]:
                    out[i * rows : (i + 1) * rows, :] = code
                    bounds[j] = jnp.where(row == i, bound, bounds[j])
                elif member == k:
                    out[i, :, :] = total
    for out, send, rows_of in zip(outs, coded, bounds):
        if send:
            out[out.shape[0] - 16 :, :] = rows_of.astype(jnp.bfloat16)


def grouped(mine, others, sends, rows):
    groups = tuple(members for _, _, members in sends)
    coded = tuple(to != O for to, _, _ in sends)
    return call(
        functools.partial(group_kernel, groups, coded),
        [mine, others],
        [
            coded_shape(len(g), rows) if s else jax.ShapeDtypeStruct((len(g), rows, rows), jnp.float32)
            for g, s in zip(groups, coded)
        ],
        moved=4 << 20,
    )


def place_kernel(tiles, place, *refs):
    ins, out = refs[:-1], refs[-1]
    c, z, x = place[2], place[3], place[4]
    rows = out.shape[0]
    for array, i, (dx, dz), turned in tiles:
        zz = (z + dz) % 4
        xx = (x + dx) % 4
        ref = ins[array]

        @pl.when(zz // 2 == c)
        def _():
            tile = ref[i, :, :] if ref.dtype == jnp.float32 else tile_of(ref, i)
            start = pl.multiple_of(((zz % 2) * 4 + xx) * rows, rows)
            out[:, pl.ds(start, rows)] = tile.T if turned else tile


O, PX, MX, PZ, MZ, F = (0, 0), (1, 0), (3, 0), (0, 1), (0, 3), (2, 2)
EARLY = ((O, O), (O, PX), (O, PZ), (MX, PX), (MZ, PZ), (MZ, PX), (PZ, PX))
LATE = ((O, F), (PX, F), (PZ, F))
EARLY_SENDS = (
    (O, False, (0, 1, 2)),
    (PX, True, (1, 3, 5, 6)),
    (PZ, True, (2, 4)),
    (MZ, False, (5,)),
    (PZ, False, (6,)),
)
LATE_SENDS = (
    (O, False, (0,)),
    (F, True, (1, 2)),
    (PX, False, (1,)),
    (PZ, False, (2,)),
)


def minus(a, b):
    return (a[0] - b[0]) % 4, (a[1] - b[1]) % 4


def local(b_factors):
    rows = b_factors.shape[0]
    flat = b_factors.reshape(rows, -1)
    aux, blk = lax.axis_index("aux"), lax.axis_index("blk")
    place = jnp.stack([blk // 16, aux // 2, aux % 2, (blk // 4) % 4, blk % 4]).astype(jnp.int32)

    own = {O: move(flat, to_own_layer)}
    for o in (PX, MX, PZ, MZ, F):
        own[o] = move(own[O], to_position(-o[0], -o[1]))
    other = {o: move(own[o], to_core) for o in (O, PX, PZ, F)}

    parts, tiles, after = [], [], ()
    for classes, sends in ((EARLY, EARLY_SENDS), (LATE, LATE_SENDS)):
        blocks = {}
        for r, q in classes:
            blocks |= {("own", r): own[r], ("own", q): own[q], ("other", q): other[q]}
        listed = [(("own", r), ("own", q), ("other", q)) for r, q in classes]
        coded = partial_tiles(place, blocks, listed, rows, after)
        after = (coded[0],)
        arrived = [move(v, to_owner(m1)) for m1, v in enumerate(coded)]
        mine = call(
            sum_kernel,
            arrived,
            jax.ShapeDtypeStruct((len(classes), rows, rows), jnp.float32),
            moved=4 << 20,
            transcendentals=1 << 21,
        )
        groups = grouped(mine, move(mine, to_core), sends, rows)
        for g, (to, turned, members) in zip(groups, sends):
            for i, k in enumerate(members):
                r, q = classes[k]
                tiles.append((len(parts), i, minus(r, q) if turned else minus(q, r), turned))
            parts.append(g if to == O else move(g, to_position(*to, swap=turned)))
    return call(
        functools.partial(place_kernel, tuple(tiles)),
        [place, *parts],
        jax.ShapeDtypeStruct((rows, 8 * rows), jnp.float32),
        moved=6 << 20,
        transcendentals=1 << 20,
    )


def solution(mesh):
    return jax.shard_map(
        local, mesh=mesh, in_specs=(P("blk", "aux", None),), out_specs=P("blk", "aux"), check_vma=False
    )
```

```python
import functools
import math

import jax
import jax.numpy as jnp
from jax import lax
from jax.experimental import pallas as pl
from jax.experimental.pallas import tpu as pltpu
from jax.sharding import PartitionSpec as P

ORDER = 32
TOP = 2.0**3.9
FLOOR = 2.0**-3.9
VMEM = 20 << 20

DEVICES = [
    (x, z, yh, yl, c)
    for yl in range(2)
    for c in range(2)
    for yh in range(2)
    for z in range(4)
    for x in range(4)
]


def move(value, where):
    index = {d: i for i, d in enumerate(DEVICES)}
    pairs = [(index[d], index[where(*d)]) for d in DEVICES]
    return lax.ppermute(value, ("aux", "blk"), pairs)


def to_own_layer(x, z, yh, yl, c):
    return x, z, c, yl, yh


def to_core(x, z, yh, yl, c):
    return x, z, yh, yl, 1 - c


def to_position(dx, dz, swap=False):
    def where(x, z, yh, yl, c):
        x, z = (x + dx) % 4, (z + dz) % 4
        return (x, z, yl, yh, c) if swap else (x, z, yh, yl, c)

    return where


def to_owner(m1):
    def where(x, z, yh, yl, c):
        return x, z, c, yl ^ m1, yh

    return where


def by_core(first, second):
    def where(x, z, yh, yl, c):
        return (second if c else first)(x, z, yh, yl, c)

    return where


def product(a, b):
    return lax.dot_general(a, b, (((1,), (1,)), ((), ())), preferred_element_type=jnp.float32)


def encode(value, bound):
    v = jnp.abs(value) * (TOP / bound) + FLOOR
    for _ in range(int(math.log2(ORDER))):
        v = v * v
    return jnp.where(value < 0, -v, v).astype(jnp.bfloat16)


def decode(code, bound):
    y = code.astype(jnp.float32)
    v = jnp.exp(jnp.log(jnp.abs(y)) * (1.0 / ORDER)) - FLOOR
    return jnp.where(y < 0, -v, v) * (bound * (1.0 / TOP))


def bound_of(top, width):
    rows = jnp.full((16, width), jnp.maximum(top, 1e-30) * 1.008, jnp.float32)
    return rows.astype(jnp.bfloat16).astype(jnp.float32)


def coded_shape(count, rows):
    return jax.ShapeDtypeStruct((count * rows + 16, rows), jnp.bfloat16)


def tile_of(ref, k):
    rows = ref.shape[1]
    bound = ref[ref.shape[0] - 16 :, :].astype(jnp.float32)[k : k + 1, :]
    return decode(ref[k * rows : (k + 1) * rows, :], bound)


def call(kernel, args, out_shape, scratch=(), any_from=None, flops=0, moved=0, transcendentals=0):
    whole = pl.BlockSpec(memory_space=pltpu.VMEM)
    specs = []
    for i, a in enumerate(args):
        if a.dtype == jnp.int32:
            specs.append(pl.BlockSpec(memory_space=pltpu.SMEM))
        else:
            specs.append(pl.BlockSpec(memory_space=pl.ANY) if any_from is not None and i >= any_from else whole)
    many = isinstance(out_shape, (list, tuple))
    return pl.pallas_call(
        kernel,
        out_shape=out_shape,
        in_specs=specs,
        out_specs=[whole] * len(out_shape) if many else whole,
        scratch_shapes=scratch,
        compiler_params=pltpu.CompilerParams(vmem_limit_bytes=VMEM),
        cost_estimate=pl.CostEstimate(flops=flops, bytes_accessed=moved, transcendentals=transcendentals),
    )(*args)


def tiles_kernel(classes, n_in, n_extra, place, *refs):
    ins = refs[:n_in]
    outs, (held, *accs, sems) = refs[n_in + n_extra : n_in + n_extra + 2], refs[n_in + n_extra + 2 :]
    yl, c = place[1], place[2]
    rows = outs[0].shape[1]
    copies = [pltpu.make_async_copy(r, held.at[i], sems.at[i]) for i, r in enumerate(ins)]
    for copy in copies:
        copy.start()
    ready = set()
    row = lax.broadcasted_iota(jnp.int32, (16, rows), 0)
    bounds = jnp.zeros((16, rows), jnp.float32)
    for k, names in enumerate(classes):
        for i in (i for pair in names for i in pair):
            if i not in ready:
                copies[i].wait()
                ready.add(i)
        acc = accs[k % 2]
        r, own, other = (i if i == j else jnp.where(c == 0, i, j) for i, j in names)
        acc[0] = product(held[r], held[own])
        acc[1] = product(held[r], held[other])
        coded = bound_of(jnp.max(jnp.abs(acc[...])), rows)
        bounds = jnp.where(row == k, coded, bounds)
        for m1, out in enumerate(outs):
            part = acc[jnp.where(yl ^ m1 == c, 0, 1)]
            out[k * rows : (k + 1) * rows, :] = encode(part, coded[0:1, :])
    for out in outs:
        out[len(classes) * rows :, :] = bounds.astype(jnp.bfloat16)


def partial_tiles(place, arrays, classes, rows, after=()):
    names = list(arrays)
    listed = tuple(tuple((names.index(i), names.index(j)) for i, j in k) for k in classes)
    depth = arrays[names[0]].shape[1]
    return call(
        functools.partial(tiles_kernel, listed, len(names), len(after)),
        [place, *arrays.values(), *after],
        [coded_shape(len(classes), rows)] * 2,
        scratch=[
            pltpu.VMEM((len(names), rows, depth), jnp.bfloat16),
            pltpu.VMEM((2, rows, rows), jnp.float32),
            pltpu.VMEM((2, rows, rows), jnp.float32),
            pltpu.SemaphoreType.DMA((len(names),)),
        ],
        any_from=1,
        flops=len(classes) * 4 * rows * rows * depth,
        moved=len(names) * rows * depth * 2,
    )


def sum_kernel(a, b, _, out):
    for k in range(out.shape[0]):
        out[k, :, :] = tile_of(a, k) + tile_of(b, k)


def group_kernel(counts, groups, *refs):
    n = 2 * len(counts)
    ins, outs = refs[:n], refs[n:]
    rows = ins[0].shape[2]
    row = lax.broadcasted_iota(jnp.int32, (16, rows), 0)
    bounds = [jnp.zeros((16, rows), jnp.float32) for _ in groups]
    first = 0
    for stage, count in enumerate(counts):
        for k in range(count):
            total = ins[2 * stage][k, :, :] + ins[2 * stage + 1][k, :, :]
            code = None
            for j, (out, (send, members)) in enumerate(zip(outs, groups)):
                for i, member in enumerate(members):
                    if member != first + k:
                        continue
                    if send:
                        if code is None:
                            bound = bound_of(jnp.max(jnp.abs(total)), rows)
                            code = encode(total, bound[0:1, :])
                        out[i * rows : (i + 1) * rows, :] = code
                        bounds[j] = jnp.where(row == i, bound, bounds[j])
                    else:
                        out[i, :, :] = total
        first += count
    for out, (send, _), rows_of in zip(outs, groups, bounds):
        if send:
            out[out.shape[0] - 16 :, :] = rows_of.astype(jnp.bfloat16)


def place_kernel(tiles, place, *refs):
    ins, out = refs[:-1], refs[-1]
    c, z, x = place[2], place[3], place[4]
    rows = out.shape[0]
    for array, i, (dx, dz), turned in tiles:
        zz = (z + dz) % 4
        xx = (x + dx) % 4
        ref = ins[array]

        @pl.when(zz // 2 == c)
        def _():
            tile = ref[i, :, :] if ref.dtype == jnp.float32 else tile_of(ref, i)
            start = pl.multiple_of(((zz % 2) * 4 + xx) * rows, rows)
            out[:, pl.ds(start, rows)] = tile.T if turned else tile


O, PX, MX, PZ, MZ, PE, ME = (0, 0), (1, 0), (3, 0), (0, 1), (0, 3), (1, 1), (3, 3)
EARLY = ((O, O), (O, PX), (O, PZ), (MX, PX), (MZ, PZ), (MZ, PX), (PZ, PX))
LATE = ((ME, PX), (ME, PZ), (ME, PE))
SENDS = (
    (O, False, (0, 1, 2)),
    (PX, True, (1, 3, 5, 6, 7)),
    (PZ, True, (2, 4, 8)),
    (ME, False, (7, 8, 9)),
    (MZ, False, (5,)),
    (PZ, False, (6,)),
)
OWN = {
    O: ("o", "o"),
    PX: ("q2", "q1"),
    PZ: ("q1", "q2"),
    MX: ("q4", "q3"),
    MZ: ("q3", "q4"),
    PE: ("pe", "pe"),
    ME: ("me", "me"),
}
OTHER = {O: ("so", "so"), PX: ("s1", "s2"), PZ: ("s2", "s1"), PE: ("spe", "spe")}


def minus(a, b):
    return (a[0] - b[0]) % 4, (a[1] - b[1]) % 4


def fetch(value, first, second):
    ways = (to_position(*minus(O, p)) for p in (first, second))
    return move(value, by_core(*ways))


def local(b_factors):
    rows = b_factors.shape[0]
    flat = b_factors.reshape(rows, -1)
    aux, blk = lax.axis_index("aux"), lax.axis_index("blk")
    place = jnp.stack([blk // 16, aux // 2, aux % 2, (blk // 4) % 4, blk % 4]).astype(jnp.int32)

    held = {"o": move(flat, to_own_layer)}
    held["q1"] = fetch(held["o"], PZ, PX)
    held["q2"] = fetch(held["o"], PX, PZ)
    held["q3"] = fetch(held["o"], MZ, MX)
    held["q4"] = fetch(held["o"], MX, MZ)
    held["pe"] = fetch(held["q1"], PX, PZ)
    held["me"] = fetch(held["q3"], MX, MZ)
    for name, source in (("so", "o"), ("s1", "q1"), ("s2", "q2")):
        held[name] = move(held[source], to_core)

    coded, after = [], ()
    for classes in (EARLY, LATE):
        if after:
            first, _ = lax.optimization_barrier((held["pe"], after[0]))
            held["spe"] = move(first, to_core)
        listed = [(OWN[r], OWN[q], OTHER[q]) for r, q in classes]
        used = {i for k in listed for pair in k for i in pair}
        arrays = {name: v for name, v in held.items() if name in used}
        coded.append(partial_tiles(place, arrays, listed, rows, after))
        after = (coded[-1][0],)

    sums = []
    for classes, stage in zip((EARLY, LATE), coded):
        mine = call(
            sum_kernel,
            [*(move(v, to_owner(m1)) for m1, v in enumerate(stage)), *after],
            jax.ShapeDtypeStruct((len(classes), rows, rows), jnp.float32),
            any_from=2,
            moved=4 << 20,
            transcendentals=1 << 21,
        )
        sums += [mine, move(mine, to_core)]

    groups = tuple((to != O, members) for to, _, members in SENDS)
    parts = call(
        functools.partial(group_kernel, (len(EARLY), len(LATE)), groups),
        sums,
        [
            coded_shape(len(g), rows) if s else jax.ShapeDtypeStruct((len(g), rows, rows), jnp.float32)
            for s, g in groups
        ],
        moved=4 << 20,
    )
    arrived, tiles = [], []
    for j, (part, (to, turned, members)) in enumerate(zip(parts, SENDS)):
        for i, k in enumerate(members):
            r, q = (EARLY + LATE)[k]
            tiles.append((j, i, minus(r, q) if turned else minus(q, r), turned))
        arrived.append(part if to == O else move(part, to_position(*to, swap=turned)))
    return call(
        functools.partial(place_kernel, tuple(tiles)),
        [place, *arrived],
        jax.ShapeDtypeStruct((rows, 8 * rows), jnp.float32),
        moved=6 << 20,
        transcendentals=1 << 20,
    )


def solution(mesh):
    return jax.shard_map(
        local, mesh=mesh, in_specs=(P("blk", "aux", None),), out_specs=P("blk", "aux"), check_vma=False
    )
```

```python
import functools
import math

import jax
import jax.numpy as jnp
from jax import lax
from jax.experimental import pallas as pl
from jax.experimental.pallas import tpu as pltpu
from jax.sharding import PartitionSpec as P

ORDER = 32
TOP = 2.0**3.9
FLOOR = 2.0**-3.9
VMEM = 20 << 20

DEVICES = [
    (x, z, yh, yl, c)
    for yl in range(2)
    for c in range(2)
    for yh in range(2)
    for z in range(4)
    for x in range(4)
]


def move(value, where):
    index = {d: i for i, d in enumerate(DEVICES)}
    pairs = [(index[d], index[where(*d)]) for d in DEVICES]
    return lax.ppermute(value, ("aux", "blk"), pairs)


def to_own_layer(x, z, yh, yl, c):
    return x, z, c, yl, yh


def to_core(x, z, yh, yl, c):
    return x, z, yh, yl, 1 - c


def to_position(dx, dz, swap=False):
    def where(x, z, yh, yl, c):
        x, z = (x + dx) % 4, (z + dz) % 4
        return (x, z, yl, yh, c) if swap else (x, z, yh, yl, c)

    return where


def to_owner(m1):
    def where(x, z, yh, yl, c):
        return x, z, c, yl ^ m1, yh

    return where


def by_core(first, second):
    def where(x, z, yh, yl, c):
        return (second if c else first)(x, z, yh, yl, c)

    return where


def product(a, b):
    return lax.dot_general(a, b, (((1,), (1,)), ((), ())), preferred_element_type=jnp.float32)


def encode(value, bound):
    v = jnp.abs(value) * (TOP / bound) + FLOOR
    for _ in range(int(math.log2(ORDER))):
        v = v * v
    return jnp.where(value < 0, -v, v).astype(jnp.bfloat16)


def decode(code, bound):
    y = code.astype(jnp.float32)
    v = jnp.exp(jnp.log(jnp.abs(y)) * (1.0 / ORDER)) - FLOOR
    return jnp.where(y < 0, -v, v) * (bound * (1.0 / TOP))


def bound_of(top, width):
    rows = jnp.full((16, width), jnp.maximum(top, 1e-30) * 1.008, jnp.float32)
    return rows.astype(jnp.bfloat16).astype(jnp.float32)


def coded_shape(count, size, width):
    return jax.ShapeDtypeStruct((count * size + 16, width), jnp.bfloat16)


def part_of(ref, k, size, start=0):
    bound = ref[ref.shape[0] - 16 :, :].astype(jnp.float32)[k : k + 1, :]
    count = size if isinstance(start, int) and start == 0 else size // 2
    return decode(ref[pl.ds(k * size + start, count), :], bound)


def call(kernel, args, out_shape, scratch=(), any_from=None, flops=0, moved=0, transcendentals=0):
    whole = pl.BlockSpec(memory_space=pltpu.VMEM)
    specs = []
    for i, a in enumerate(args):
        if a.dtype == jnp.int32:
            specs.append(pl.BlockSpec(memory_space=pltpu.SMEM))
        else:
            specs.append(pl.BlockSpec(memory_space=pl.ANY) if any_from is not None and i >= any_from else whole)
    many = isinstance(out_shape, (list, tuple))
    return pl.pallas_call(
        kernel,
        out_shape=out_shape,
        in_specs=specs,
        out_specs=[whole] * len(out_shape) if many else whole,
        scratch_shapes=scratch,
        compiler_params=pltpu.CompilerParams(vmem_limit_bytes=VMEM),
        cost_estimate=pl.CostEstimate(flops=flops, bytes_accessed=moved, transcendentals=transcendentals),
    )(*args)


def tiles_kernel(classes, n_in, n_extra, place, *refs):
    ins = refs[:n_in]
    outs, (held, *accs, sems) = refs[n_in + n_extra : n_in + n_extra + 2], refs[n_in + n_extra + 2 :]
    yl, c = place[1], place[2]
    rows = outs[0].shape[1]
    copies = [pltpu.make_async_copy(r, held.at[i], sems.at[i]) for i, r in enumerate(ins)]
    for copy in copies:
        copy.start()
    ready = set()
    row = lax.broadcasted_iota(jnp.int32, (16, rows), 0)
    bounds = jnp.zeros((16, rows), jnp.float32)
    for k, names in enumerate(classes):
        for i in (i for pair in names for i in pair):
            if i not in ready:
                copies[i].wait()
                ready.add(i)
        acc = accs[k % 2]
        r, own, other = (i if i == j else jnp.where(c == 0, i, j) for i, j in names)
        acc[0] = product(held[r], held[own])
        acc[1] = product(held[r], held[other])
        coded = bound_of(jnp.max(jnp.abs(acc[...])), rows)
        bounds = jnp.where(row == k, coded, bounds)
        for m1, out in enumerate(outs):
            part = acc[jnp.where(yl ^ m1 == c, 0, 1)]
            out[k * rows : (k + 1) * rows, :] = encode(part, coded[0:1, :])
    for out in outs:
        out[len(classes) * rows :, :] = bounds.astype(jnp.bfloat16)


def partial_tiles(place, arrays, classes, rows, after=()):
    names = list(arrays)
    listed = tuple(tuple((names.index(i), names.index(j)) for i, j in k) for k in classes)
    depth = arrays[names[0]].shape[1]
    return call(
        functools.partial(tiles_kernel, listed, len(names), len(after)),
        [place, *arrays.values(), *after],
        [coded_shape(len(classes), rows, rows)] * 2,
        scratch=[
            pltpu.VMEM((len(names), rows, depth), jnp.bfloat16),
            pltpu.VMEM((2, rows, rows), jnp.float32),
            pltpu.VMEM((2, rows, rows), jnp.float32),
            pltpu.SemaphoreType.DMA((len(names),)),
        ],
        any_from=1,
        flops=len(classes) * 4 * rows * rows * depth,
        moved=len(names) * rows * depth * 2,
    )


def sum_kernel(whole, place, a, b, _, *outs):
    c = place[2]
    rows = a.shape[1]
    half = rows // 2
    kept, given = outs[-2], outs[-1]
    count = (a.shape[0] - 16) // rows
    for k in range(count):
        if k < whole:
            outs[0][k, :, :] = part_of(a, k, rows) + part_of(b, k, rows)
        else:
            for out, h in ((kept, c), (given, 1 - c)):
                start = pl.multiple_of(h * half, half)
                out[k - whole, :, :] = part_of(a, k, rows, start) + part_of(b, k, rows, start)


def group_kernel(classes, groups, place, *refs):
    ins, outs = refs[: len(refs) - len(groups)], refs[len(refs) - len(groups) :]
    width = outs[0].shape[1]
    half = width // 2
    start = pl.multiple_of(place[2] * half, half)
    row = lax.broadcasted_iota(jnp.int32, (16, width), 0)
    bounds = [jnp.zeros((16, width), jnp.float32) for _ in groups]
    for k, (pair, i) in classes.items():
        rows = pl.ds(start, half) if ins[2 * pair].shape[1] == width else pl.ds(0, half)
        total = ins[2 * pair][i, rows, :] + ins[2 * pair + 1][i, rows, :]
        bound = bound_of(jnp.max(jnp.abs(total)), width)
        code = encode(total, bound[0:1, :])
        for j, (out, members) in enumerate(zip(outs, groups)):
            for i, member in enumerate(members):
                if member == k:
                    out[i * half : (i + 1) * half, :] = code
                    bounds[j] = jnp.where(row == i, bound, bounds[j])
    for out, rows_of in zip(outs, bounds):
        out[out.shape[0] - 16 :, :] = rows_of.astype(jnp.bfloat16)


def place_kernel(stay, tiles, n, place, *refs):
    sums, own, other, out = refs[:2], refs[2 : 2 + n], refs[2 + n : 2 + 2 * n], refs[2 + 2 * n]
    c, z, x = place[2], place[3], place[4]
    rows = out.shape[0]
    half = rows // 2
    first = pl.multiple_of(c * half, half)
    second = pl.multiple_of((1 - c) * half, half)

    def at(d, write):
        dx, dz = d
        zz = (z + dz) % 4
        xx = (x + dx) % 4

        @pl.when(zz // 2 == c)
        def _():
            write(pl.multiple_of(((zz % 2) * 4 + xx) * rows, rows))

    for i, d in stay:

        def write(start, i=i):
            out[:, pl.ds(start, rows)] = sums[0][i, :, :] + sums[1][i, :, :]

        at(d, write)
    for array, i, d, turned in tiles:

        def write(start, array=array, i=i, turned=turned):
            for ref, offset in ((own[array], first), (other[array], second)):
                tile = part_of(ref, i, half)
                if turned:
                    out[:, pl.ds(pl.multiple_of(start + offset, half), half)] = tile.T
                else:
                    out[pl.ds(offset, half), pl.ds(start, rows)] = tile

        at(d, write)


O, PX, MX, PZ, MZ, PE, ME = (0, 0), (1, 0), (3, 0), (0, 1), (0, 3), (1, 1), (3, 3)
EARLY = ((O, O), (O, PX), (O, PZ), (MX, PX), (MZ, PZ), (MZ, PX), (PZ, PX))
LATE = ((ME, PX), (ME, PZ), (ME, PE))
STAY = 3
SENDS = (
    (PX, True, (1, 3, 5, 6, 7)),
    (PZ, True, (2, 8)),
    (ME, False, (7, 8, 9)),
    (MZ, False, (4, 5)),
    (PZ, False, (6,)),
)
OWN = {
    O: ("o", "o"),
    PX: ("q2", "q1"),
    PZ: ("q1", "q2"),
    MX: ("q4", "q3"),
    MZ: ("q3", "q4"),
    PE: ("pe", "pe"),
    ME: ("me", "me"),
}
OTHER = {O: ("so", "so"), PX: ("s1", "s2"), PZ: ("s2", "s1"), PE: ("spe", "spe")}


def minus(a, b):
    return (a[0] - b[0]) % 4, (a[1] - b[1]) % 4


def fetch(value, first, second):
    ways = (to_position(*minus(O, p)) for p in (first, second))
    return move(value, by_core(*ways))


def local(b_factors):
    rows = b_factors.shape[0]
    flat = b_factors.reshape(rows, -1)
    aux, blk = lax.axis_index("aux"), lax.axis_index("blk")
    place = jnp.stack([blk // 16, aux // 2, aux % 2, (blk // 4) % 4, blk % 4]).astype(jnp.int32)

    held = {"o": move(flat, to_own_layer)}
    held["q1"] = fetch(held["o"], PZ, PX)
    held["q2"] = fetch(held["o"], PX, PZ)
    held["q3"] = fetch(held["o"], MZ, MX)
    held["q4"] = fetch(held["o"], MX, MZ)
    held["pe"] = fetch(held["q1"], PX, PZ)
    held["me"] = fetch(held["q3"], MX, MZ)
    for name, source in (("so", "o"), ("s1", "q1"), ("s2", "q2")):
        held[name] = move(held[source], to_core)

    coded, after = [], ()
    for classes in (EARLY, LATE):
        if after:
            first, _ = lax.optimization_barrier((held["pe"], after[0]))
            held["spe"] = move(first, to_core)
        listed = [(OWN[r], OWN[q], OTHER[q]) for r, q in classes]
        used = {i for k in listed for pair in k for i in pair}
        arrays = {name: v for name, v in held.items() if name in used}
        coded.append(partial_tiles(place, arrays, listed, rows, after))
        after = (coded[-1][0],)

    sums = []
    for classes, stage, whole, weight in zip((EARLY, LATE), coded, (STAY, 0), (1, 10**11)):
        halves = jax.ShapeDtypeStruct((len(classes) - whole, rows // 2, rows), jnp.float32)
        full = [jax.ShapeDtypeStruct((whole, rows, rows), jnp.float32)] * (whole > 0)
        *full, kept, given = call(
            functools.partial(sum_kernel, whole),
            [place, *(move(v, to_owner(m1)) for m1, v in enumerate(stage)), *after],
            [*full, halves, halves],
            any_from=3,
            flops=weight,
            moved=weight,
            transcendentals=weight,
        )
        sums += [v for f in full for v in (f, move(f, to_core))] + [kept, move(given, to_core)]

    where = {k: (0, k) for k in range(1, STAY)}
    where |= {k: (1, k - STAY) for k in range(STAY, len(EARLY))}
    where |= {len(EARLY) + k: (2, k) for k in range(len(LATE))}
    groups = tuple(members for _, _, members in SENDS)
    parts = call(
        functools.partial(group_kernel, where, groups),
        [place, *sums],
        [coded_shape(len(g), rows // 2, rows) for g in groups],
        moved=4 << 20,
    )
    own, tiles = [], []
    for j, (part, (to, turned, members)) in enumerate(zip(parts, SENDS)):
        for i, k in enumerate(members):
            r, q = (EARLY + LATE)[k]
            tiles.append((j, i, minus(r, q) if turned else minus(q, r), turned))
        own.append(move(part, to_position(*to, swap=turned)))
    own = lax.optimization_barrier(own)
    other = [move(v, to_core) for v in own]
    stay = tuple((k, minus(q, r)) for k, (r, q) in enumerate(EARLY[:STAY]))
    return call(
        functools.partial(place_kernel, stay, tuple(tiles), len(own)),
        [place, *sums[:2], *own, *other],
        jax.ShapeDtypeStruct((rows, 8 * rows), jnp.float32),
        moved=6 << 20,
        transcendentals=1 << 20,
    )


def solution(mesh):
    return jax.shard_map(
        local, mesh=mesh, in_specs=(P("blk", "aux", None),), out_specs=P("blk", "aux"), check_vma=False
    )
```

```python
import functools
import math

import jax
import jax.numpy as jnp
from jax import lax
from jax.experimental import pallas as pl
from jax.experimental.pallas import tpu as pltpu
from jax.sharding import PartitionSpec as P

ORDER = 32
TOP = 2.0**3.9
FLOOR = 2.0**-3.9
VMEM = 20 << 20

DEVICES = [
    (x, z, yh, yl, c)
    for yl in range(2)
    for c in range(2)
    for yh in range(2)
    for z in range(4)
    for x in range(4)
]


def move(value, where):
    index = {d: i for i, d in enumerate(DEVICES)}
    pairs = [(index[d], index[where(*d)]) for d in DEVICES]
    return lax.ppermute(value, ("aux", "blk"), pairs)


def to_own_layer(x, z, yh, yl, c):
    return x, z, c, yl, yh


def to_core(x, z, yh, yl, c):
    return x, z, yh, yl, 1 - c


def to_position(dx, dz, swap=False):
    def where(x, z, yh, yl, c):
        x, z = (x + dx) % 4, (z + dz) % 4
        return (x, z, yl, yh, c) if swap else (x, z, yh, yl, c)

    return where


def to_owner(m1):
    def where(x, z, yh, yl, c):
        return x, z, c, yl ^ m1, yh

    return where


def by_core(first, second):
    def where(x, z, yh, yl, c):
        return (second if c else first)(x, z, yh, yl, c)

    return where


def product(a, b):
    return lax.dot_general(a, b, (((1,), (1,)), ((), ())), preferred_element_type=jnp.float32)


def encode(value, bound):
    v = jnp.abs(value) * (TOP / bound) + FLOOR
    for _ in range(int(math.log2(ORDER))):
        v = v * v
    return jnp.where(value < 0, -v, v).astype(jnp.bfloat16)


def decode(code, bound):
    y = code.astype(jnp.float32)
    v = jnp.exp(jnp.log(jnp.abs(y)) * (1.0 / ORDER)) - FLOOR
    return jnp.where(y < 0, -v, v) * (bound * (1.0 / TOP))


def bound_of(top, width):
    rows = jnp.full((16, width), jnp.maximum(top, 1e-30) * 1.008, jnp.float32)
    return rows.astype(jnp.bfloat16).astype(jnp.float32)


def coded_shape(count, size, width):
    return jax.ShapeDtypeStruct((count * size + 16, width), jnp.bfloat16)


def part_of(ref, k, size, start=0):
    bound = ref[ref.shape[0] - 16 :, :].astype(jnp.float32)[k : k + 1, :]
    count = size if isinstance(start, int) and start == 0 else size // 2
    return decode(ref[pl.ds(k * size + start, count), :], bound)


def call(kernel, args, out_shape, scratch=(), any_from=None, flops=0, moved=0, transcendentals=0, vmem=VMEM, out_any=False):
    whole = pl.BlockSpec(memory_space=pltpu.VMEM)
    specs = []
    for i, a in enumerate(args):
        if a.dtype == jnp.int32:
            specs.append(pl.BlockSpec(memory_space=pltpu.SMEM))
        else:
            specs.append(pl.BlockSpec(memory_space=pl.ANY) if any_from is not None and i >= any_from else whole)
    many = isinstance(out_shape, (list, tuple))
    return pl.pallas_call(
        kernel,
        out_shape=out_shape,
        in_specs=specs,
        out_specs=[whole] * len(out_shape) if many else pl.BlockSpec(memory_space=pl.ANY) if out_any else whole,
        scratch_shapes=scratch,
        compiler_params=pltpu.CompilerParams(vmem_limit_bytes=vmem),
        cost_estimate=pl.CostEstimate(flops=flops, bytes_accessed=moved, transcendentals=transcendentals),
    )(*args)


def tiles_kernel(classes, n_in, n_extra, place, *refs):
    ins = refs[:n_in]
    outs, (held, *accs, sems) = refs[n_in + n_extra : n_in + n_extra + 2], refs[n_in + n_extra + 2 :]
    yl, c = place[1], place[2]
    rows = outs[0].shape[1]
    copies = [pltpu.make_async_copy(r, held.at[i], sems.at[i]) for i, r in enumerate(ins)]
    for copy in copies:
        copy.start()
    ready = set()
    row = lax.broadcasted_iota(jnp.int32, (16, rows), 0)
    bounds = jnp.zeros((16, rows), jnp.float32)
    for k, names in enumerate(classes):
        for i in (i for pair in names for i in pair):
            if i not in ready:
                copies[i].wait()
                ready.add(i)
        acc = accs[k % 2]
        r, own, other = (i if i == j else jnp.where(c == 0, i, j) for i, j in names)
        acc[0] = product(held[r], held[own])
        acc[1] = product(held[r], held[other])
        coded = bound_of(jnp.max(jnp.abs(acc[...])), rows)
        bounds = jnp.where(row == k, coded, bounds)
        for m1, out in zip((1, 0), outs):
            part = acc[jnp.where(yl ^ m1 == c, 0, 1)]
            out[k * rows : (k + 1) * rows, :] = encode(part, coded[0:1, :])
    for out in outs:
        out[len(classes) * rows :, :] = bounds.astype(jnp.bfloat16)


def partial_tiles(place, arrays, classes, rows, after=()):
    names = list(arrays)
    listed = tuple(tuple((names.index(i), names.index(j)) for i, j in k) for k in classes)
    depth = arrays[names[0]].shape[1]
    return call(
        functools.partial(tiles_kernel, listed, len(names), len(after)),
        [place, *arrays.values(), *after],
        [coded_shape(len(classes), rows, rows)] * 2,
        scratch=[
            pltpu.VMEM((len(names), rows, depth), jnp.bfloat16),
            pltpu.VMEM((2, rows, rows), jnp.float32),
            pltpu.VMEM((2, rows, rows), jnp.float32),
            pltpu.SemaphoreType.DMA((len(names),)),
        ],
        any_from=1,
        flops=len(classes) * 4 * rows * rows * depth,
        moved=len(names) * rows * depth * 2,
    )


def sum_kernel(whole, place, a, b, _, *outs):
    c = place[2]
    rows = a.shape[1]
    half = rows // 2
    full, kept, given = outs
    count = (a.shape[0] - 16) // rows
    for k in range(count):
        if k < whole:
            full[k, :, :] = part_of(a, k, rows) + part_of(b, k, rows)
        else:
            for out, h in ((kept, c), (given, 1 - c)):
                start = pl.multiple_of(h * half, half)
                out[k - whole, :, :] = part_of(a, k, rows, start) + part_of(b, k, rows, start)


def group_kernel(classes, groups, place, *refs):
    ins, outs = refs[: len(refs) - len(groups)], refs[len(refs) - len(groups) :]
    width = outs[0].shape[1]
    half = width // 2
    start = pl.multiple_of(place[2] * half, half)
    row = lax.broadcasted_iota(jnp.int32, (16, width), 0)
    bounds = [jnp.zeros((16, width), jnp.float32) for _ in groups]
    for k, (pair, i) in classes.items():
        rows = pl.ds(start, half) if ins[2 * pair].shape[1] == width else pl.ds(0, half)
        total = ins[2 * pair][i, rows, :] + ins[2 * pair + 1][i, rows, :]
        bound = bound_of(jnp.max(jnp.abs(total)), width)
        code = encode(total, bound[0:1, :])
        for j, (out, members) in enumerate(zip(outs, groups)):
            for i, member in enumerate(members):
                if member == k:
                    out[i * half : (i + 1) * half, :] = code
                    bounds[j] = jnp.where(row == i, bound, bounds[j])
    for out, rows_of in zip(outs, bounds):
        out[out.shape[0] - 16 :, :] = rows_of.astype(jnp.bfloat16)


def place_kernel(stay, tiles, n, place, *refs):
    own, other, sums = refs[:n], refs[n : 2 * n], refs[2 * n : 2 * n + 4]
    out, result, early, late, in_sems, out_sem = refs[2 * n + 4 :]
    held = (early, late)
    c, z, x = place[2], place[3], place[4]
    rows = result.shape[0]
    half = rows // 2
    first = pl.multiple_of(c * half, half)
    second = pl.multiple_of((1 - c) * half, half)
    arriving = [pltpu.make_async_copy(v, held[i // 2].at[i % 2], in_sems.at[i]) for i, v in enumerate(sums)]
    for copy in arriving:
        copy.start()

    def at(d, write):
        dx, dz = d
        zz = (z + dz) % 4
        xx = (x + dx) % 4

        @pl.when(zz // 2 == c)
        def _():
            start = pl.multiple_of(((zz % 2) * 4 + xx) * rows, rows)
            write(start)
            columns = pl.ds(start, rows)
            pltpu.make_async_copy(result.at[:, columns], out.at[:, columns], out_sem).start()

    for array, i, d, turned in tiles:

        def write(start, array=array, i=i, turned=turned):
            for ref, offset in ((own[array], first), (other[array], second)):
                tile = part_of(ref, i, half)
                if turned:
                    result[:, pl.ds(pl.multiple_of(start + offset, half), half)] = tile.T
                else:
                    result[pl.ds(offset, half), pl.ds(start, rows)] = tile

        at(d, write)
    for copy in arriving:
        copy.wait()
    for stage, i, d in stay:

        def write(start, stage=stage, i=i):
            result[:, pl.ds(start, rows)] = held[stage][0, i, :, :] + held[stage][1, i, :, :]

        at(d, write)
    pltpu.make_async_copy(result, out, out_sem).wait()


O, PX, MX, PZ, MZ, PE, ME = (0, 0), (1, 0), (3, 0), (0, 1), (0, 3), (1, 1), (3, 3)
EARLY = ((O, PX), (O, PZ), (MX, PX), (MZ, PZ), (MZ, PX), (PZ, PX))
LATE = ((O, O), (ME, PX), (ME, PZ), (ME, PE))
CLASSES = EARLY + LATE
STAY = (2, 1)
SENDS = (
    (PX, True, (0, 2, 4, 5, 7)),
    (PZ, True, (1, 8)),
    (ME, False, (7, 8, 9)),
    (MZ, False, (3, 4)),
    (PZ, False, (5,)),
)
OWN = {
    O: ("o", "o"),
    PX: ("q2", "q1"),
    PZ: ("q1", "q2"),
    MX: ("q4", "q3"),
    MZ: ("q3", "q4"),
    PE: ("pe", "pe"),
    ME: ("me", "me"),
}
OTHER = {O: ("so", "so"), PX: ("s1", "s2"), PZ: ("s2", "s1"), PE: ("spe", "spe")}


def minus(a, b):
    return (a[0] - b[0]) % 4, (a[1] - b[1]) % 4


def fetch(value, first, second):
    ways = (to_position(*minus(O, p)) for p in (first, second))
    return move(value, by_core(*ways))


def local(b_factors):
    rows = b_factors.shape[0]
    flat = b_factors.reshape(rows, -1)
    aux, blk = lax.axis_index("aux"), lax.axis_index("blk")
    place = jnp.stack([blk // 16, aux // 2, aux % 2, (blk // 4) % 4, blk % 4]).astype(jnp.int32)

    held = {"o": move(flat, to_own_layer)}
    held["q1"] = fetch(held["o"], PZ, PX)
    held["q2"] = fetch(held["o"], PX, PZ)
    held["q3"] = fetch(held["o"], MZ, MX)
    held["q4"] = fetch(held["o"], MX, MZ)
    held["pe"] = fetch(held["q1"], PX, PZ)
    held["me"] = fetch(held["q3"], MX, MZ)
    for name, source in (("s1", "q1"), ("s2", "q2")):
        held[name] = move(held[source], to_core)

    coded, after = [], ()
    for classes in (EARLY, LATE):
        if after:
            first, second, _ = lax.optimization_barrier((held["o"], held["pe"], after[0]))
            held["so"] = move(first, to_core)
            held["spe"] = move(second, to_core)
        listed = [(OWN[r], OWN[q], OTHER[q]) for r, q in classes]
        used = {i for k in listed for pair in k for i in pair}
        arrays = {name: v for name, v in held.items() if name in used}
        coded.append(partial_tiles(place, arrays, listed, rows, after))
        after = (coded[-1][0],)

    sums = []
    for classes, stage, whole, weight in zip((EARLY, LATE), coded, STAY, (1, 10**11)):
        halves = jax.ShapeDtypeStruct((len(classes) - whole, rows // 2, rows), jnp.float32)
        full = jax.ShapeDtypeStruct((whole, rows, rows), jnp.float32)
        full, kept, given = call(
            functools.partial(sum_kernel, whole),
            [place, *(move(v, to_owner(m1)) for m1, v in zip((1, 0), stage)), *after],
            [full, halves, halves],
            any_from=3,
            flops=weight,
            moved=weight,
            transcendentals=weight,
        )
        sums += [full, move(full, to_core), kept, move(given, to_core)]

    where = {}
    for stage, (classes, whole) in enumerate(zip((EARLY, LATE), STAY)):
        for k in range(len(classes)):
            pair = (2 * stage, k) if k < whole else (2 * stage + 1, k - whole)
            where[len(where)] = pair
    sent = {k: where[k] for k in range(len(CLASSES)) if any(k in m for _, _, m in SENDS)}
    groups = tuple(members for _, _, members in SENDS)
    parts = call(
        functools.partial(group_kernel, sent, groups),
        [place, *sums],
        [coded_shape(len(g), rows // 2, rows) for g in groups],
        moved=4 << 20,
    )
    own, tiles = [], []
    for j, (part, (to, turned, members)) in enumerate(zip(parts, SENDS)):
        for i, k in enumerate(members):
            r, q = CLASSES[k]
            tiles.append((j, i, minus(r, q) if turned else minus(q, r), turned))
        own.append(move(part, to_position(*to, swap=turned)))
    own = lax.optimization_barrier(own)
    other = [move(v, to_core) for v in own]
    stay = tuple(
        (where[k][0] // 2, where[k][1], minus(q, r)) for k, (r, q) in enumerate(CLASSES) if where[k][0] % 2 == 0
    )
    return call(
        functools.partial(place_kernel, stay, tuple(tiles), len(own)),
        [place, *own, *other, *sums[:2], *sums[4:6]],
        jax.ShapeDtypeStruct((rows, 8 * rows), jnp.float32),
        scratch=[
            pltpu.VMEM((rows, 8 * rows), jnp.float32),
            *(pltpu.VMEM((2, n, rows, rows), jnp.float32) for n in STAY),
            pltpu.SemaphoreType.DMA((4,)),
            pltpu.SemaphoreType.DMA,
        ],
        any_from=1 + 2 * len(own),
        out_any=True,
        moved=6 << 20,
    )


def solution(mesh):
    return jax.shard_map(
        local, mesh=mesh, in_specs=(P("blk", "aux", None),), out_specs=P("blk", "aux"), check_vma=False
    )
```

```python
import functools
import math

import jax
import jax.numpy as jnp
from jax import lax
from jax.experimental import pallas as pl
from jax.experimental.pallas import tpu as pltpu
from jax.sharding import PartitionSpec as P

ORDER = 32
TOP = 2.0**3.9
FLOOR = 2.0**-3.9
VMEM = 20 << 20

DEVICES = [
    (x, z, yh, yl, c)
    for yl in range(2)
    for c in range(2)
    for yh in range(2)
    for z in range(4)
    for x in range(4)
]


def move(value, where):
    index = {d: i for i, d in enumerate(DEVICES)}
    pairs = [(index[d], index[where(*d)]) for d in DEVICES]
    return lax.ppermute(value, ("aux", "blk"), pairs)


def to_own_layer(x, z, yh, yl, c):
    return x, z, c, yl, yh


def to_core(x, z, yh, yl, c):
    return x, z, yh, yl, 1 - c


def to_position(dx, dz, swap=False):
    def where(x, z, yh, yl, c):
        x, z = (x + dx) % 4, (z + dz) % 4
        return (x, z, yl, yh, c) if swap else (x, z, yh, yl, c)

    return where


def to_owner(m1, m2=0):
    def where(x, z, yh, yl, c):
        return x, z, c, yl ^ m1, yh ^ m2

    return where


def by_core(first, second):
    def where(x, z, yh, yl, c):
        return (second if c else first)(x, z, yh, yl, c)

    return where


def product(a, b):
    return lax.dot_general(a, b, (((1,), (1,)), ((), ())), preferred_element_type=jnp.float32)


def encode(value, bound):
    v = jnp.abs(value) * (TOP / bound) + FLOOR
    for _ in range(int(math.log2(ORDER))):
        v = v * v
    return jnp.where(value < 0, -v, v).astype(jnp.bfloat16)


def decode(code, bound):
    y = code.astype(jnp.float32)
    v = jnp.exp(jnp.log(jnp.abs(y)) * (1.0 / ORDER)) - FLOOR
    return jnp.where(y < 0, -v, v) * (bound * (1.0 / TOP))


def bound_of(top, width):
    rows = jnp.full((16, width), jnp.maximum(top, 1e-30) * 1.008, jnp.float32)
    return rows.astype(jnp.bfloat16).astype(jnp.float32)


def coded_shape(count, size, width):
    return jax.ShapeDtypeStruct((count * size + 16, width), jnp.bfloat16)


def part_of(ref, k, size, start=0):
    bound = ref[ref.shape[0] - 16 :, :].astype(jnp.float32)[k : k + 1, :]
    count = size if isinstance(start, int) and start == 0 else size // 2
    return decode(ref[pl.ds(k * size + start, count), :], bound)


def call(kernel, args, out_shape, scratch=(), any_from=None, flops=0, moved=0, transcendentals=0, vmem=VMEM, out_any=False):
    whole = pl.BlockSpec(memory_space=pltpu.VMEM)
    specs = []
    for i, a in enumerate(args):
        if a.dtype == jnp.int32:
            specs.append(pl.BlockSpec(memory_space=pltpu.SMEM))
        else:
            specs.append(pl.BlockSpec(memory_space=pl.ANY) if any_from is not None and i >= any_from else whole)
    many = isinstance(out_shape, (list, tuple))
    return pl.pallas_call(
        kernel,
        out_shape=out_shape,
        in_specs=specs,
        out_specs=[whole] * len(out_shape) if many else pl.BlockSpec(memory_space=pl.ANY) if out_any else whole,
        scratch_shapes=scratch,
        compiler_params=pltpu.CompilerParams(vmem_limit_bytes=vmem),
        cost_estimate=pl.CostEstimate(flops=flops, bytes_accessed=moved, transcendentals=transcendentals),
    )(*args)


WHOLE = ((1, 0), (0, 0))
SPLIT = ((1, 0), (1, 1), (0, 0), (0, 1))


def tiles_kernel(classes, split, n_in, n_extra, place, *refs):
    ins = refs[:n_in]
    n_out = 4 if split else 2
    outs, (held, *accs, sems) = refs[n_in + n_extra :][:n_out], refs[n_in + n_extra + n_out :]
    yh, yl, c = place[0], place[1], place[2]
    rows = outs[0].shape[1]
    size = rows // 2 if split else rows
    copies = [pltpu.make_async_copy(r, held.at[i], sems.at[i]) for i, r in enumerate(ins)]
    for copy in copies:
        copy.start()
    ready = set()
    row = lax.broadcasted_iota(jnp.int32, (16, rows), 0)
    bounds = jnp.zeros((16, rows), jnp.float32)
    for k, names in enumerate(classes):
        for i in (i for pair in names for i in pair):
            if i not in ready:
                copies[i].wait()
                ready.add(i)
        acc = accs[k % 2]
        r, own, other = (i if i == j else jnp.where(c == 0, i, j) for i, j in names)
        acc[0] = product(held[r], held[own])
        acc[1] = product(held[r], held[other])
        coded = bound_of(jnp.max(jnp.abs(acc[...])), rows)
        bounds = jnp.where(row == k, coded, bounds)
        for (m1, m2), out in zip(SPLIT if split else WHOLE, outs):
            part = jnp.where(yl ^ m1 == c, 0, 1)
            start = pl.multiple_of((yh ^ m2) * size, size) if split else 0
            out[k * size : (k + 1) * size, :] = encode(acc[part, pl.ds(start, size), :], coded[0:1, :])
    for out in outs:
        out[len(classes) * size :, :] = bounds.astype(jnp.bfloat16)


def partial_tiles(place, arrays, classes, split, rows, after=()):
    names = list(arrays)
    listed = tuple(tuple((names.index(i), names.index(j)) for i, j in k) for k in classes)
    depth = arrays[names[0]].shape[1]
    return call(
        functools.partial(tiles_kernel, listed, split, len(names), len(after)),
        [place, *arrays.values(), *after],
        [coded_shape(len(classes), rows // 2 if split else rows, rows)] * (4 if split else 2),
        scratch=[
            pltpu.VMEM((len(names), rows, depth), jnp.bfloat16),
            pltpu.VMEM((2, rows, rows), jnp.float32),
            pltpu.VMEM((2, rows, rows), jnp.float32),
            pltpu.SemaphoreType.DMA((len(names),)),
        ],
        any_from=1,
        flops=len(classes) * 4 * rows * rows * depth,
        moved=len(names) * rows * depth * 2,
    )


def sum_kernel(members, place, a, b, _, kept, given):
    c = place[2]
    rows = a.shape[1]
    half = rows // 2
    for i, k in enumerate(members):
        for out, h in ((kept, c), (given, 1 - c)):
            start = pl.multiple_of(h * half, half)
            out[i, :, :] = part_of(a, k, rows, start) + part_of(b, k, rows, start)


def whole_sum_kernel(a, b, _, out):
    rows = a.shape[1]
    for k in range(out.shape[0]):
        out[k, :, :] = part_of(a, k, rows) + part_of(b, k, rows)


def half_sum_kernel(a, b, c, d, out):
    half = a.shape[1] // 2
    for k in range(out.shape[0]):
        out[k, :, :] = (part_of(a, k, half) + part_of(b, k, half)) + (part_of(c, k, half) + part_of(d, k, half))


def group_kernel(early, groups, kept, given, late, *outs):
    half, width = kept.shape[1:]
    row = lax.broadcasted_iota(jnp.int32, (16, width), 0)
    bounds = [jnp.zeros((16, width), jnp.float32) for _ in groups]
    for k in range(len(CLASSES)):
        if k in early:
            i = early.index(k)
            total = kept[i, :, :] + given[i, :, :]
        elif k >= len(EARLY):
            total = late[k - len(EARLY), :, :]
        else:
            continue
        bound = bound_of(jnp.max(jnp.abs(total)), width)
        code = encode(total, bound[0:1, :])
        for j, (out, members) in enumerate(zip(outs, groups)):
            for i, member in enumerate(members):
                if member == k:
                    out[i * half : (i + 1) * half, :] = code
                    bounds[j] = jnp.where(row == i, bound, bounds[j])
    for out, rows_of in zip(outs, bounds):
        out[out.shape[0] - 16 :, :] = rows_of.astype(jnp.bfloat16)


def place_kernel(stay, tiles, n, place, *refs):
    own, other, sums = refs[:n], refs[n : 2 * n], refs[2 * n : 2 * n + 2]
    out, result, held, in_sems, out_sem = refs[2 * n + 2 :]
    c, z, x = place[2], place[3], place[4]
    rows = result.shape[0]
    half = rows // 2
    first = pl.multiple_of(c * half, half)
    second = pl.multiple_of((1 - c) * half, half)
    arriving = [pltpu.make_async_copy(v, held.at[i], in_sems.at[i]) for i, v in enumerate(sums)]
    for copy in arriving:
        copy.start()

    def at(d, write):
        dx, dz = d
        zz = (z + dz) % 4
        xx = (x + dx) % 4

        @pl.when(zz // 2 == c)
        def _():
            start = pl.multiple_of(((zz % 2) * 4 + xx) * rows, rows)
            write(start)
            columns = pl.ds(start, rows)
            pltpu.make_async_copy(result.at[:, columns], out.at[:, columns], out_sem).start()

    for array, i, d, turned in tiles:

        def write(start, array=array, i=i, turned=turned):
            for ref, offset in ((own[array], first), (other[array], second)):
                tile = part_of(ref, i, half)
                if turned:
                    result[:, pl.ds(pl.multiple_of(start + offset, half), half)] = tile.T
                else:
                    result[pl.ds(offset, half), pl.ds(start, rows)] = tile

        at(d, write)
    for copy in arriving:
        copy.wait()
    for i, d in stay:

        def write(start, i=i):
            result[:, pl.ds(start, rows)] = held[0, i, :, :] + held[1, i, :, :]

        at(d, write)
    pltpu.make_async_copy(result, out, out_sem).wait()


O, PX, MX, PZ, MZ, PE, ME = (0, 0), (1, 0), (3, 0), (0, 1), (0, 3), (1, 1), (3, 3)
EARLY = ((O, PX), (O, PZ), (O, O), (MX, PX), (MZ, PZ), (MZ, PX), (PZ, PX))
LATE = ((ME, PX), (ME, PZ), (ME, PE))
CLASSES = EARLY + LATE
STAY = 3
SENDS = (
    (PX, True, (0, 3, 5, 6, 7)),
    (PZ, True, (1, 8)),
    (ME, False, (7, 8, 9)),
    (MZ, False, (4, 5)),
    (PZ, False, (6,)),
)
OWN = {
    O: ("o", "o"),
    PX: ("q2", "q1"),
    PZ: ("q1", "q2"),
    MX: ("q4", "q3"),
    MZ: ("q3", "q4"),
    PE: ("pe", "pe"),
    ME: ("me", "me"),
}
OTHER = {O: ("so", "so"), PX: ("s1", "s2"), PZ: ("s2", "s1"), PE: ("spe", "spe")}


def minus(a, b):
    return (a[0] - b[0]) % 4, (a[1] - b[1]) % 4


def fetch(value, first, second):
    ways = (to_position(*minus(O, p)) for p in (first, second))
    return move(value, by_core(*ways))


def local(b_factors):
    rows = b_factors.shape[0]
    flat = b_factors.reshape(rows, -1)
    aux, blk = lax.axis_index("aux"), lax.axis_index("blk")
    place = jnp.stack([blk // 16, aux // 2, aux % 2, (blk // 4) % 4, blk % 4]).astype(jnp.int32)

    held = {"o": move(flat, to_own_layer)}
    held["q1"] = fetch(held["o"], PZ, PX)
    held["q2"] = fetch(held["o"], PX, PZ)
    held["q3"] = fetch(held["o"], MZ, MX)
    held["q4"] = fetch(held["o"], MX, MZ)
    held["pe"] = fetch(held["q1"], PX, PZ)
    held["me"] = fetch(held["q3"], MX, MZ)
    for name, source in (("s1", "q1"), ("s2", "q2")):
        held[name] = move(held[source], to_core)
    held["so"] = move(lax.optimization_barrier((held["o"], held["q4"]))[0], to_core)

    coded, after = [], ()
    for classes in (EARLY, LATE):
        if after:
            first, _ = lax.optimization_barrier((held["pe"], after[0]))
            held["spe"] = move(first, to_core)
        listed = [(OWN[r], OWN[q], OTHER[q]) for r, q in classes]
        used = {i for k in listed for pair in k for i in pair}
        arrays = {name: v for name, v in held.items() if name in used}
        coded.append(partial_tiles(place, arrays, listed, bool(after), rows, after))
        after = (coded[-1][0],)

    groups = tuple(members for _, _, members in SENDS)
    early = tuple(k for k in range(len(EARLY)) if any(k in g for g in groups))
    arrived = [move(v, to_owner(*m)) for m, v in zip(WHOLE, coded[0])]
    kept, given = call(
        functools.partial(sum_kernel, early),
        [place, *arrived, *after],
        [jax.ShapeDtypeStruct((len(early), rows // 2, rows), jnp.float32)] * 2,
        any_from=3,
        flops=1,
        moved=1,
    )
    weight = 10**11
    late = call(
        half_sum_kernel,
        [move(v, to_owner(*m)) for m, v in zip(SPLIT, coded[1])],
        jax.ShapeDtypeStruct((len(LATE), rows // 2, rows), jnp.float32),
        flops=weight,
        moved=weight,
        transcendentals=weight,
    )
    parts = list(
        call(
            functools.partial(group_kernel, early, groups),
            [kept, move(given, to_core), late],
            [coded_shape(len(g), rows // 2, rows) for g in groups],
            moved=4 << 20,
        )
    )
    full = call(
        whole_sum_kernel,
        [*arrived, parts[0]],
        jax.ShapeDtypeStruct((STAY, rows, rows), jnp.float32),
        any_from=2,
        flops=1,
        moved=1,
    )
    parts[3], other_full = lax.optimization_barrier((parts[3], move(full, to_core)))
    own, tiles = [], []
    for j, (part, (to, turned, members)) in enumerate(zip(parts, SENDS)):
        for i, k in enumerate(members):
            r, q = CLASSES[k]
            tiles.append((j, i, minus(r, q) if turned else minus(q, r), turned))
        own.append(move(part, to_position(*to, swap=turned)))
    own = lax.optimization_barrier(own)
    other = [move(v, to_core) for v in own]
    stay = tuple((k, minus(q, r)) for k, (r, q) in enumerate(CLASSES[:STAY]))
    return call(
        functools.partial(place_kernel, stay, tuple(tiles), len(own)),
        [place, *own, *other, full, other_full],
        jax.ShapeDtypeStruct((rows, 8 * rows), jnp.float32),
        scratch=[
            pltpu.VMEM((rows, 8 * rows), jnp.float32),
            pltpu.VMEM((2, STAY, rows, rows), jnp.float32),
            pltpu.SemaphoreType.DMA((2,)),
            pltpu.SemaphoreType.DMA,
        ],
        any_from=1 + 2 * len(own),
        out_any=True,
        moved=6 << 20,
    )


def solution(mesh):
    return jax.shard_map(
        local, mesh=mesh, in_specs=(P("blk", "aux", None),), out_specs=P("blk", "aux"), check_vma=False
    )
```

```python
import functools
import math

import jax
import jax.numpy as jnp
from jax import lax
from jax.experimental import pallas as pl
from jax.experimental.pallas import tpu as pltpu
from jax.sharding import PartitionSpec as P

ORDER = 32
TOP = 2.0**3.9
FLOOR = 2.0**-3.9
VMEM = 20 << 20

DEVICES = [
    (x, z, yh, yl, c)
    for yl in range(2)
    for c in range(2)
    for yh in range(2)
    for z in range(4)
    for x in range(4)
]


def move(value, where):
    index = {d: i for i, d in enumerate(DEVICES)}
    pairs = [(index[d], index[where(*d)]) for d in DEVICES]
    return lax.ppermute(value, ("aux", "blk"), pairs)


def to_own_layer(x, z, yh, yl, c):
    return x, z, c, yl, yh


def to_core(x, z, yh, yl, c):
    return x, z, yh, yl, 1 - c


def to_position(dx, dz, swap=False):
    def where(x, z, yh, yl, c):
        x, z = (x + dx) % 4, (z + dz) % 4
        return (x, z, yl, yh, c) if swap else (x, z, yh, yl, c)

    return where


def to_owner(m1, m2=0):
    def where(x, z, yh, yl, c):
        return x, z, c, yl ^ m1, yh ^ m2

    return where


def by_core(first, second):
    def where(x, z, yh, yl, c):
        return (second if c else first)(x, z, yh, yl, c)

    return where


def product(a, b):
    return lax.dot_general(a, b, (((1,), (1,)), ((), ())), preferred_element_type=jnp.float32)


def encode(value, bound):
    v = jnp.abs(value) * (TOP / bound) + FLOOR
    for _ in range(int(math.log2(ORDER))):
        v = v * v
    return jnp.where(value < 0, -v, v).astype(jnp.bfloat16)


def decode(code, bound):
    y = code.astype(jnp.float32)
    v = jnp.exp(jnp.log(jnp.abs(y)) * (1.0 / ORDER)) - FLOOR
    return jnp.where(y < 0, -v, v) * (bound * (1.0 / TOP))


def bound_of(top, width):
    rows = jnp.full((16, width), jnp.maximum(top, 1e-30) * 1.008, jnp.float32)
    return rows.astype(jnp.bfloat16).astype(jnp.float32)


def coded_shape(count, size, width):
    return jax.ShapeDtypeStruct((count * size + 16, width), jnp.bfloat16)


def part_of(ref, k, size, start=0):
    bound = ref[ref.shape[0] - 16 :, :].astype(jnp.float32)[k : k + 1, :]
    count = size if isinstance(start, int) and start == 0 else size // 2
    return decode(ref[pl.ds(k * size + start, count), :], bound)


def call(kernel, args, out_shape, scratch=(), any_from=None, flops=0, moved=0, transcendentals=0, vmem=VMEM, out_any=False):
    whole = pl.BlockSpec(memory_space=pltpu.VMEM)
    specs = []
    for i, a in enumerate(args):
        if a.dtype == jnp.int32:
            specs.append(pl.BlockSpec(memory_space=pltpu.SMEM))
        else:
            specs.append(pl.BlockSpec(memory_space=pl.ANY) if any_from is not None and i >= any_from else whole)
    many = isinstance(out_shape, (list, tuple))
    return pl.pallas_call(
        kernel,
        out_shape=out_shape,
        in_specs=specs,
        out_specs=[whole] * len(out_shape) if many else pl.BlockSpec(memory_space=pl.ANY) if out_any else whole,
        scratch_shapes=scratch,
        compiler_params=pltpu.CompilerParams(vmem_limit_bytes=vmem),
        cost_estimate=pl.CostEstimate(flops=flops, bytes_accessed=moved, transcendentals=transcendentals),
    )(*args)


WHOLE = ((1, 0), (0, 0))
SPLIT = ((1, 0), (1, 1), (0, 0), (0, 1))


def tiles_kernel(classes, split, pieces, n_extra, place, *refs):
    n_in = sum(pieces)
    ins = refs[:n_in]
    n_out = 4 if split else 2
    outs, (held, *accs, sems) = refs[n_in + n_extra :][:n_out], refs[n_in + n_extra + n_out :]
    yh, yl, c = place[0], place[1], place[2]
    rows = outs[0].shape[1]
    size = rows // 2 if split else rows
    copies, at = [], 0
    for i, n in enumerate(pieces):
        part = rows // n
        copies.append(
            [
                pltpu.make_async_copy(ins[at + j], held.at[i, j * part : (j + 1) * part], sems.at[at + j])
                for j in range(n)
            ]
        )
        at += n
    for group in copies:
        for copy in group:
            copy.start()
    ready = set()
    row = lax.broadcasted_iota(jnp.int32, (16, rows), 0)
    bounds = jnp.zeros((16, rows), jnp.float32)
    for k, names in enumerate(classes):
        for i in (i for pair in names for i in pair):
            if i not in ready:
                for copy in copies[i]:
                    copy.wait()
                ready.add(i)
        acc = accs[k % 2]
        r, own, other = (i if i == j else jnp.where(c == 0, i, j) for i, j in names)
        acc[0] = product(held[r], held[own])
        acc[1] = product(held[r], held[other])
        coded = bound_of(jnp.max(jnp.abs(acc[...])), rows)
        bounds = jnp.where(row == k, coded, bounds)
        for (m1, m2), out in zip(SPLIT if split else WHOLE, outs):
            part = jnp.where(yl ^ m1 == c, 0, 1)
            start = pl.multiple_of((yh ^ m2) * size, size) if split else 0
            out[k * size : (k + 1) * size, :] = encode(acc[part, pl.ds(start, size), :], coded[0:1, :])
    for out in outs:
        out[len(classes) * size :, :] = bounds.astype(jnp.bfloat16)


def partial_tiles(place, arrays, classes, split, rows, after=()):
    names = list(arrays)
    listed = tuple(tuple((names.index(i), names.index(j)) for i, j in k) for k in classes)
    pieces = tuple(len(v) for v in arrays.values())
    blocks = [v for p in arrays.values() for v in p]
    depth = blocks[0].shape[1]
    return call(
        functools.partial(tiles_kernel, listed, split, pieces, len(after)),
        [place, *blocks, *after],
        [coded_shape(len(classes), rows // 2 if split else rows, rows)] * (4 if split else 2),
        scratch=[
            pltpu.VMEM((len(names), rows, depth), jnp.bfloat16),
            pltpu.VMEM((2, rows, rows), jnp.float32),
            pltpu.VMEM((2, rows, rows), jnp.float32),
            pltpu.SemaphoreType.DMA((len(blocks),)),
        ],
        any_from=1,
        flops=len(classes) * 4 * rows * rows * depth,
        moved=len(names) * rows * depth * 2,
    )


def sum_kernel(members, place, a, b, _, kept, given):
    c = place[2]
    rows = a.shape[1]
    half = rows // 2
    for i, k in enumerate(members):
        for out, h in ((kept, c), (given, 1 - c)):
            start = pl.multiple_of(h * half, half)
            out[i, :, :] = part_of(a, k, rows, start) + part_of(b, k, rows, start)


def whole_sum_kernel(a, b, _, out):
    rows = a.shape[1]
    for k in range(out.shape[0]):
        out[k, :, :] = part_of(a, k, rows) + part_of(b, k, rows)


def half_sum_kernel(a, b, c, d, out):
    half = a.shape[1] // 2
    for k in range(out.shape[0]):
        out[k, :, :] = (part_of(a, k, half) + part_of(b, k, half)) + (part_of(c, k, half) + part_of(d, k, half))


def group_kernel(early, groups, kept, given, late, *outs):
    half, width = kept.shape[1:]
    row = lax.broadcasted_iota(jnp.int32, (16, width), 0)
    bounds = [jnp.zeros((16, width), jnp.float32) for _ in groups]
    for k in range(len(CLASSES)):
        if k in early:
            i = early.index(k)
            total = kept[i, :, :] + given[i, :, :]
        elif k >= len(EARLY):
            total = late[k - len(EARLY), :, :]
        else:
            continue
        bound = bound_of(jnp.max(jnp.abs(total)), width)
        code = encode(total, bound[0:1, :])
        for j, (out, members) in enumerate(zip(outs, groups)):
            for i, member in enumerate(members):
                if member == k:
                    out[i * half : (i + 1) * half, :] = code
                    bounds[j] = jnp.where(row == i, bound, bounds[j])
    for out, rows_of in zip(outs, bounds):
        out[out.shape[0] - 16 :, :] = rows_of.astype(jnp.bfloat16)


def place_kernel(stay, tiles, n, place, *refs):
    own, other, sums = refs[:n], refs[n : 2 * n], refs[2 * n : 2 * n + 2]
    out, result, held, in_sems, out_sem = refs[2 * n + 2 :]
    c, z, x = place[2], place[3], place[4]
    rows = result.shape[0]
    half = rows // 2
    first = pl.multiple_of(c * half, half)
    second = pl.multiple_of((1 - c) * half, half)
    arriving = [pltpu.make_async_copy(v, held.at[i], in_sems.at[i]) for i, v in enumerate(sums)]
    for copy in arriving:
        copy.start()

    def at(d, write):
        dx, dz = d
        zz = (z + dz) % 4
        xx = (x + dx) % 4

        @pl.when(zz // 2 == c)
        def _():
            start = pl.multiple_of(((zz % 2) * 4 + xx) * rows, rows)
            write(start)
            columns = pl.ds(start, rows)
            pltpu.make_async_copy(result.at[:, columns], out.at[:, columns], out_sem).start()

    for array, i, d, turned in tiles:

        def write(start, array=array, i=i, turned=turned):
            for ref, offset in ((own[array], first), (other[array], second)):
                tile = part_of(ref, i, half)
                if turned:
                    result[:, pl.ds(pl.multiple_of(start + offset, half), half)] = tile.T
                else:
                    result[pl.ds(offset, half), pl.ds(start, rows)] = tile

        at(d, write)
    for copy in arriving:
        copy.wait()
    for i, d in stay:

        def write(start, i=i):
            result[:, pl.ds(start, rows)] = held[0, i, :, :] + held[1, i, :, :]

        at(d, write)
    pltpu.make_async_copy(result, out, out_sem).wait()


O, PX, MX, PZ, MZ, PE, ME = (0, 0), (1, 0), (3, 0), (0, 1), (0, 3), (1, 1), (3, 3)
EARLY = ((O, PX), (O, PZ), (O, O), (MX, PX), (MZ, PZ), (MZ, PX), (PZ, PX))
LATE = ((ME, PX), (ME, PZ), (ME, PE))
CLASSES = EARLY + LATE
STAY = 3
SENDS = (
    (PX, True, (0, 3, 5, 6, 7)),
    (PZ, True, (1, 8)),
    (ME, False, (7, 8, 9)),
    (MZ, False, (4, 5)),
    (PZ, False, (6,)),
)
OWN = {
    O: ("o", "o"),
    PX: ("q2", "q1"),
    PZ: ("q1", "q2"),
    MX: ("q4", "q3"),
    MZ: ("q3", "q4"),
    PE: ("pe", "pe"),
    ME: ("me", "me"),
}
OTHER = {O: ("so", "so"), PX: ("s1", "s2"), PZ: ("s2", "s1"), PE: ("spe", "spe")}


def minus(a, b):
    return (a[0] - b[0]) % 4, (a[1] - b[1]) % 4


def fetch(value, first, second):
    ways = (to_position(*minus(O, p)) for p in (first, second))
    return move(value, by_core(*ways))


def local(b_factors):
    rows = b_factors.shape[0]
    flat = b_factors.reshape(rows, -1)
    aux, blk = lax.axis_index("aux"), lax.axis_index("blk")
    place = jnp.stack([blk // 16, aux // 2, aux % 2, (blk // 4) % 4, blk % 4]).astype(jnp.int32)

    held = {"o": move(flat, to_own_layer)}
    held["q1"] = fetch(held["o"], PZ, PX)
    held["q2"] = fetch(held["o"], PX, PZ)
    held["q3"] = fetch(held["o"], MZ, MX)
    held["q4"] = fetch(held["o"], MX, MZ)
    held["pe"] = fetch(held["q1"], PX, PZ)
    held["me"] = fetch(held["q3"], MX, MZ)
    for name, source in (("s1", "q1"), ("s2", "q2")):
        held[name] = move(held[source], to_core)
    held["so"] = move(lax.optimization_barrier((held["o"], held["q1"]))[0], to_core)

    coded, after = [], ()
    for classes in (EARLY, LATE):
        if after:
            first, _ = lax.optimization_barrier((held["pe"], after[0]))
            half = rows // 2
            held["spe"] = (move(first[:half], to_core), move(first[half:], to_core))
        listed = [(OWN[r], OWN[q], OTHER[q]) for r, q in classes]
        used = {i for k in listed for pair in k for i in pair}
        arrays = {name: v if isinstance(v, tuple) else (v,) for name, v in held.items() if name in used}
        coded.append(partial_tiles(place, arrays, listed, bool(after), rows, after))
        after = (coded[-1][0],)

    groups = tuple(members for _, _, members in SENDS)
    early = tuple(k for k in range(len(EARLY)) if any(k in g for g in groups))
    arrived = [move(v, to_owner(*m)) for m, v in zip(WHOLE, coded[0])]
    kept, given = call(
        functools.partial(sum_kernel, early),
        [place, *arrived, *after],
        [jax.ShapeDtypeStruct((len(early), rows // 2, rows), jnp.float32)] * 2,
        any_from=3,
        flops=1,
        moved=1,
    )
    weight = 10**11
    late = call(
        half_sum_kernel,
        [move(v, to_owner(*m)) for m, v in zip(SPLIT, coded[1])],
        jax.ShapeDtypeStruct((len(LATE), rows // 2, rows), jnp.float32),
        flops=weight,
        moved=weight,
        transcendentals=weight,
    )
    parts = list(
        call(
            functools.partial(group_kernel, early, groups),
            [kept, move(given, to_core), late],
            [coded_shape(len(g), rows // 2, rows) for g in groups],
            moved=4 << 20,
        )
    )
    full = call(
        whole_sum_kernel,
        [*arrived, parts[0]],
        jax.ShapeDtypeStruct((STAY, rows, rows), jnp.float32),
        any_from=2,
        flops=1,
        moved=1,
    )
    parts[3], other_full = lax.optimization_barrier((parts[3], move(full, to_core)))
    own, tiles = [], []
    for j, (part, (to, turned, members)) in enumerate(zip(parts, SENDS)):
        for i, k in enumerate(members):
            r, q = CLASSES[k]
            tiles.append((j, i, minus(r, q) if turned else minus(q, r), turned))
        own.append(move(part, to_position(*to, swap=turned)))
    own = lax.optimization_barrier(own)
    other = [move(v, to_core) for v in own]
    stay = tuple((k, minus(q, r)) for k, (r, q) in enumerate(CLASSES[:STAY]))
    return call(
        functools.partial(place_kernel, stay, tuple(tiles), len(own)),
        [place, *own, *other, full, other_full],
        jax.ShapeDtypeStruct((rows, 8 * rows), jnp.float32),
        scratch=[
            pltpu.VMEM((rows, 8 * rows), jnp.float32),
            pltpu.VMEM((2, STAY, rows, rows), jnp.float32),
            pltpu.SemaphoreType.DMA((2,)),
            pltpu.SemaphoreType.DMA,
        ],
        any_from=1 + 2 * len(own),
        out_any=True,
        moved=6 << 20,
    )


def solution(mesh):
    return jax.shard_map(
        local, mesh=mesh, in_specs=(P("blk", "aux", None),), out_specs=P("blk", "aux"), check_vma=False
    )
```

```python
import functools
import math

import jax
import jax.numpy as jnp
from jax import lax
from jax.experimental import pallas as pl
from jax.experimental.pallas import tpu as pltpu
from jax.sharding import PartitionSpec as P

ORDER = 32
TOP = 2.0**3.9
FLOOR = 2.0**-3.9
VMEM = 20 << 20

DEVICES = [
    (x, z, yh, yl, c)
    for yl in range(2)
    for c in range(2)
    for yh in range(2)
    for z in range(4)
    for x in range(4)
]


def move(value, where):
    index = {d: i for i, d in enumerate(DEVICES)}
    pairs = [(index[d], index[where(*d)]) for d in DEVICES]
    return lax.ppermute(value, ("aux", "blk"), pairs)


def to_own_layer(x, z, yh, yl, c):
    return x, z, c, yl, yh


def to_core(x, z, yh, yl, c):
    return x, z, yh, yl, 1 - c


def to_position(dx, dz, swap=False):
    def where(x, z, yh, yl, c):
        x, z = (x + dx) % 4, (z + dz) % 4
        return (x, z, yl, yh, c) if swap else (x, z, yh, yl, c)

    return where


def to_owner(m1, m2=0):
    def where(x, z, yh, yl, c):
        return x, z, c, yl ^ m1, yh ^ m2

    return where


def by_core(first, second):
    def where(x, z, yh, yl, c):
        return (second if c else first)(x, z, yh, yl, c)

    return where


def product(a, b):
    return lax.dot_general(a, b, (((1,), (1,)), ((), ())), preferred_element_type=jnp.float32)


def encode(value, bound):
    v = jnp.abs(value) * (TOP / bound) + FLOOR
    for _ in range(int(math.log2(ORDER))):
        v = v * v
    return jnp.where(value < 0, -v, v).astype(jnp.bfloat16)


def decode(code, bound):
    y = code.astype(jnp.float32)
    v = jnp.exp(jnp.log(jnp.abs(y)) * (1.0 / ORDER)) - FLOOR
    return jnp.where(y < 0, -v, v) * (bound * (1.0 / TOP))


def bound_of(top, width):
    rows = jnp.full((16, width), jnp.maximum(top, 1e-30) * 1.008, jnp.float32)
    return rows.astype(jnp.bfloat16).astype(jnp.float32)


def coded_shape(count, size, width):
    return jax.ShapeDtypeStruct((count * size + 16, width), jnp.bfloat16)


def part_of(ref, k, size, start=0):
    bound = ref[ref.shape[0] - 16 :, :].astype(jnp.float32)[k : k + 1, :]
    count = size if isinstance(start, int) and start == 0 else size // 2
    return decode(ref[pl.ds(k * size + start, count), :], bound)


def call(kernel, args, out_shape, scratch=(), any_from=None, flops=0, moved=0, transcendentals=0, vmem=VMEM, out_any=False):
    whole = pl.BlockSpec(memory_space=pltpu.VMEM)
    specs = []
    for i, a in enumerate(args):
        if a.dtype == jnp.int32:
            specs.append(pl.BlockSpec(memory_space=pltpu.SMEM))
        else:
            specs.append(pl.BlockSpec(memory_space=pl.ANY) if any_from is not None and i >= any_from else whole)
    many = isinstance(out_shape, (list, tuple))
    return pl.pallas_call(
        kernel,
        out_shape=out_shape,
        in_specs=specs,
        out_specs=[whole] * len(out_shape) if many else pl.BlockSpec(memory_space=pl.ANY) if out_any else whole,
        scratch_shapes=scratch,
        compiler_params=pltpu.CompilerParams(vmem_limit_bytes=vmem),
        cost_estimate=pl.CostEstimate(flops=flops, bytes_accessed=moved, transcendentals=transcendentals),
    )(*args)


WHOLE = ((1, 0), (0, 0))
SPLIT = ((1, 0), (1, 1), (0, 0), (0, 1))


def tiles_kernel(classes, split, pieces, n_extra, place, *refs):
    n_in = sum(pieces)
    ins = refs[:n_in]
    n_out = 4 if split else 2
    outs, (held, *accs, sems) = refs[n_in + n_extra :][:n_out], refs[n_in + n_extra + n_out :]
    yh, yl, c = place[0], place[1], place[2]
    rows = outs[0].shape[1]
    size = rows // 2 if split else rows
    copies, at = [], 0
    for i, n in enumerate(pieces):
        part = rows // n
        copies.append(
            [
                pltpu.make_async_copy(ins[at + j], held.at[i, j * part : (j + 1) * part], sems.at[at + j])
                for j in range(n)
            ]
        )
        at += n
    for group in copies:
        for copy in group:
            copy.start()
    ready = set()
    row = lax.broadcasted_iota(jnp.int32, (16, rows), 0)
    bounds = jnp.zeros((16, rows), jnp.float32)
    for k, names in enumerate(classes):
        for i in (i for pair in names for i in pair):
            if i not in ready:
                for copy in copies[i]:
                    copy.wait()
                ready.add(i)
        acc = accs[k % 2]
        r, own, other = (i if i == j else jnp.where(c == 0, i, j) for i, j in names)
        acc[0] = product(held[r], held[own])
        acc[1] = product(held[r], held[other])
        coded = bound_of(jnp.max(jnp.abs(acc[...])), rows)
        bounds = jnp.where(row == k, coded, bounds)
        for (m1, m2), out in zip(SPLIT if split else WHOLE, outs):
            part = jnp.where(yl ^ m1 == c, 0, 1)
            start = pl.multiple_of((yh ^ m2) * size, size) if split else 0
            out[k * size : (k + 1) * size, :] = encode(acc[part, pl.ds(start, size), :], coded[0:1, :])
    for out in outs:
        out[len(classes) * size :, :] = bounds.astype(jnp.bfloat16)


def partial_tiles(place, arrays, classes, split, rows, after=()):
    names = list(arrays)
    listed = tuple(tuple((names.index(i), names.index(j)) for i, j in k) for k in classes)
    pieces = tuple(len(v) for v in arrays.values())
    blocks = [v for p in arrays.values() for v in p]
    depth = blocks[0].shape[1]
    return call(
        functools.partial(tiles_kernel, listed, split, pieces, len(after)),
        [place, *blocks, *after],
        [coded_shape(len(classes), rows // 2 if split else rows, rows)] * (4 if split else 2),
        scratch=[
            pltpu.VMEM((len(names), rows, depth), jnp.bfloat16),
            pltpu.VMEM((2, rows, rows), jnp.float32),
            pltpu.VMEM((2, rows, rows), jnp.float32),
            pltpu.SemaphoreType.DMA((len(blocks),)),
        ],
        any_from=1,
        flops=len(classes) * 4 * rows * rows * depth,
        moved=len(names) * rows * depth * 2,
    )


def sum_kernel(members, place, a, b, _, kept, given):
    c = place[2]
    rows = a.shape[1]
    half = rows // 2
    for i, k in enumerate(members):
        for out, h in ((kept, c), (given, 1 - c)):
            start = pl.multiple_of(h * half, half)
            out[i, :, :] = part_of(a, k, rows, start) + part_of(b, k, rows, start)


def whole_sum_kernel(a, b, _, out):
    rows = a.shape[1]
    for k in range(out.shape[0]):
        out[k, :, :] = part_of(a, k, rows) + part_of(b, k, rows)


def half_sum_kernel(a, b, c, d, _, out):
    half = a.shape[1] // 2
    for k in range(out.shape[0]):
        out[k, :, :] = (part_of(a, k, half) + part_of(b, k, half)) + (part_of(c, k, half) + part_of(d, k, half))


def group_kernel(early, groups, kept, given, late, *outs):
    half, width = kept.shape[1:]
    row = lax.broadcasted_iota(jnp.int32, (16, width), 0)
    bounds = [jnp.zeros((16, width), jnp.float32) for _ in groups]
    for k in range(len(CLASSES)):
        if k in early:
            i = early.index(k)
            total = kept[i, :, :] + given[i, :, :]
        elif k >= len(EARLY):
            total = late[k - len(EARLY), :, :]
        else:
            continue
        bound = bound_of(jnp.max(jnp.abs(total)), width)
        code = encode(total, bound[0:1, :])
        for j, (out, members) in enumerate(zip(outs, groups)):
            for i, member in enumerate(members):
                if member == k:
                    out[i * half : (i + 1) * half, :] = code
                    bounds[j] = jnp.where(row == i, bound, bounds[j])
    for out, rows_of in zip(outs, bounds):
        out[out.shape[0] - 16 :, :] = rows_of.astype(jnp.bfloat16)


def place_kernel(stay, tiles, n, place, *refs):
    own, other, sums = refs[:n], refs[n : 2 * n], refs[2 * n : 2 * n + 2]
    out, result, held, in_sems, out_sem = refs[2 * n + 2 :]
    c, z, x = place[2], place[3], place[4]
    rows = result.shape[0]
    half = rows // 2
    first = pl.multiple_of(c * half, half)
    second = pl.multiple_of((1 - c) * half, half)
    arriving = [pltpu.make_async_copy(v, held.at[i], in_sems.at[i]) for i, v in enumerate(sums)]
    for copy in arriving:
        copy.start()

    def at(d, write):
        dx, dz = d
        zz = (z + dz) % 4
        xx = (x + dx) % 4

        @pl.when(zz // 2 == c)
        def _():
            start = pl.multiple_of(((zz % 2) * 4 + xx) * rows, rows)
            write(start)
            columns = pl.ds(start, rows)
            pltpu.make_async_copy(result.at[:, columns], out.at[:, columns], out_sem).start()

    for array, i, d, turned in tiles:

        def write(start, array=array, i=i, turned=turned):
            for ref, offset in ((own[array], first), (other[array], second)):
                tile = part_of(ref, i, half)
                if turned:
                    result[:, pl.ds(pl.multiple_of(start + offset, half), half)] = tile.T
                else:
                    result[pl.ds(offset, half), pl.ds(start, rows)] = tile

        at(d, write)
    for copy in arriving:
        copy.wait()
    for i, d in stay:

        def write(start, i=i):
            result[:, pl.ds(start, rows)] = held[0, i, :, :] + held[1, i, :, :]

        at(d, write)
    pltpu.make_async_copy(result, out, out_sem).wait()


O, PX, MX, PZ, MZ, PE, ME = (0, 0), (1, 0), (3, 0), (0, 1), (0, 3), (1, 1), (3, 3)
EARLY = ((O, PX), (O, PZ), (O, O), (MX, PX), (MZ, PZ), (MZ, PX), (PZ, PX))
LATE = ((ME, PX), (ME, PZ), (ME, PE))
CLASSES = EARLY + LATE
STAY = 3
SENDS = (
    (PX, True, (0, 3, 5, 6, 7)),
    (PZ, True, (1, 8)),
    (ME, False, (7, 8, 9)),
    (MZ, False, (4, 5)),
    (PZ, False, (6,)),
)
OWN = {
    O: ("o", "o"),
    PX: ("q2", "q1"),
    PZ: ("q1", "q2"),
    MX: ("q4", "q3"),
    MZ: ("q3", "q4"),
    PE: ("pe", "pe"),
    ME: ("me", "me"),
}
OTHER = {O: ("so", "so"), PX: ("s1", "s2"), PZ: ("s2", "s1"), PE: ("spe", "spe")}


def minus(a, b):
    return (a[0] - b[0]) % 4, (a[1] - b[1]) % 4


def fetch(value, first, second):
    ways = (to_position(*minus(O, p)) for p in (first, second))
    return move(value, by_core(*ways))


def local(b_factors):
    rows = b_factors.shape[0]
    flat = b_factors.reshape(rows, -1)
    aux, blk = lax.axis_index("aux"), lax.axis_index("blk")
    place = jnp.stack([blk // 16, aux // 2, aux % 2, (blk // 4) % 4, blk % 4]).astype(jnp.int32)

    held = {"o": move(flat, to_own_layer)}
    held["q1"] = fetch(held["o"], PZ, PX)
    held["q2"] = fetch(held["o"], PX, PZ)
    held["q3"] = fetch(held["o"], MZ, MX)
    held["q4"] = fetch(held["o"], MX, MZ)
    held["pe"] = fetch(held["q1"], PX, PZ)
    held["me"] = fetch(held["q3"], MX, MZ)
    for name, source in (("s1", "q1"), ("s2", "q2")):
        held[name] = move(held[source], to_core)
    held["so"] = move(lax.optimization_barrier((held["o"], held["q1"]))[0], to_core)

    coded, after = [], ()
    for classes in (EARLY, LATE):
        if after:
            first, _ = lax.optimization_barrier((held["pe"], after[0]))
            half = rows // 2
            held["spe"] = (move(first[:half], to_core), move(first[half:], to_core))
        listed = [(OWN[r], OWN[q], OTHER[q]) for r, q in classes]
        used = {i for k in listed for pair in k for i in pair}
        arrays = {name: v if isinstance(v, tuple) else (v,) for name, v in held.items() if name in used}
        coded.append(partial_tiles(place, arrays, listed, bool(after), rows, after))
        after = (coded[-1][0],)

    groups = tuple(members for _, _, members in SENDS)
    early = tuple(k for k in range(len(EARLY)) if any(k in g for g in groups))
    arrived = [move(v, to_owner(*m)) for m, v in zip(WHOLE, coded[0])]
    kept, given = call(
        functools.partial(sum_kernel, early),
        [place, *arrived, *after],
        [jax.ShapeDtypeStruct((len(early), rows // 2, rows), jnp.float32)] * 2,
        any_from=3,
        flops=1,
        moved=1,
    )
    full = call(
        whole_sum_kernel,
        [*arrived, kept],
        jax.ShapeDtypeStruct((STAY, rows, rows), jnp.float32),
        any_from=2,
        flops=1,
        moved=1,
    )
    weight = 10**11
    late = call(
        half_sum_kernel,
        [*(move(v, to_owner(*m)) for m, v in zip(SPLIT, coded[1])), full],
        jax.ShapeDtypeStruct((len(LATE), rows // 2, rows), jnp.float32),
        any_from=4,
        flops=weight,
        moved=weight,
        transcendentals=weight,
    )
    parts = list(
        call(
            functools.partial(group_kernel, early, groups),
            [kept, move(given, to_core), late],
            [coded_shape(len(g), rows // 2, rows) for g in groups],
            moved=4 << 20,
        )
    )
    parts[3], other_full = lax.optimization_barrier((parts[3], move(full, to_core)))
    own, tiles = [], []
    for j, (part, (to, turned, members)) in enumerate(zip(parts, SENDS)):
        for i, k in enumerate(members):
            r, q = CLASSES[k]
            tiles.append((j, i, minus(r, q) if turned else minus(q, r), turned))
        own.append(move(part, to_position(*to, swap=turned)))
    own = lax.optimization_barrier(own)
    other = [move(v, to_core) for v in own]
    stay = tuple((k, minus(q, r)) for k, (r, q) in enumerate(CLASSES[:STAY]))
    return call(
        functools.partial(place_kernel, stay, tuple(tiles), len(own)),
        [place, *own, *other, full, other_full],
        jax.ShapeDtypeStruct((rows, 8 * rows), jnp.float32),
        scratch=[
            pltpu.VMEM((rows, 8 * rows), jnp.float32),
            pltpu.VMEM((2, STAY, rows, rows), jnp.float32),
            pltpu.SemaphoreType.DMA((2,)),
            pltpu.SemaphoreType.DMA,
        ],
        any_from=1 + 2 * len(own),
        out_any=True,
        moved=6 << 20,
    )


def solution(mesh):
    return jax.shard_map(
        local, mesh=mesh, in_specs=(P("blk", "aux", None),), out_specs=P("blk", "aux"), check_vma=False
    )
```

```python
import functools
import math

import jax
import jax.numpy as jnp
from jax import lax
from jax.experimental import pallas as pl
from jax.experimental.pallas import tpu as pltpu
from jax.sharding import PartitionSpec as P

ORDER = 32
TOP = 2.0**3.9
FLOOR = 2.0**-3.9
VMEM = 20 << 20

DEVICES = [
    (x, z, yh, yl, c)
    for yl in range(2)
    for c in range(2)
    for yh in range(2)
    for z in range(4)
    for x in range(4)
]


def move(value, where):
    index = {d: i for i, d in enumerate(DEVICES)}
    pairs = [(index[d], index[where(*d)]) for d in DEVICES]
    return lax.ppermute(value, ("aux", "blk"), pairs)


def to_own_layer(x, z, yh, yl, c):
    return x, z, c, yl, yh


def to_core(x, z, yh, yl, c):
    return x, z, yh, yl, 1 - c


def to_position(dx, dz, swap=False):
    def where(x, z, yh, yl, c):
        x, z = (x + dx) % 4, (z + dz) % 4
        return (x, z, yl, yh, c) if swap else (x, z, yh, yl, c)

    return where


def to_owner(m1, m2=0):
    def where(x, z, yh, yl, c):
        return x, z, c, yl ^ m1, yh ^ m2

    return where


def by_core(first, second):
    def where(x, z, yh, yl, c):
        return (second if c else first)(x, z, yh, yl, c)

    return where


def product(a, b):
    return lax.dot_general(a, b, (((1,), (1,)), ((), ())), preferred_element_type=jnp.float32)


def encode(value, bound):
    v = jnp.abs(value) * (TOP / bound) + FLOOR
    for _ in range(int(math.log2(ORDER))):
        v = v * v
    return jnp.where(value < 0, -v, v).astype(jnp.bfloat16)


def decode(code, bound):
    y = code.astype(jnp.float32)
    v = jnp.exp(jnp.log(jnp.abs(y)) * (1.0 / ORDER)) - FLOOR
    return jnp.where(y < 0, -v, v) * (bound * (1.0 / TOP))


def bound_of(top, width):
    rows = jnp.full((16, width), jnp.maximum(top, 1e-30) * 1.008, jnp.float32)
    return rows.astype(jnp.bfloat16).astype(jnp.float32)


def coded_shape(count, size, width):
    return jax.ShapeDtypeStruct((count * size + 16, width), jnp.bfloat16)


def part_of(ref, k, size, start=0):
    bound = ref[ref.shape[0] - 16 :, :].astype(jnp.float32)[k : k + 1, :]
    count = size if isinstance(start, int) and start == 0 else size // 2
    return decode(ref[pl.ds(k * size + start, count), :], bound)


def call(kernel, args, out_shape, scratch=(), any_from=None, flops=0, moved=0, transcendentals=0, vmem=VMEM, out_any=False):
    whole = pl.BlockSpec(memory_space=pltpu.VMEM)
    specs = []
    for i, a in enumerate(args):
        if a.dtype == jnp.int32:
            specs.append(pl.BlockSpec(memory_space=pltpu.SMEM))
        else:
            specs.append(pl.BlockSpec(memory_space=pl.ANY) if any_from is not None and i >= any_from else whole)
    many = isinstance(out_shape, (list, tuple))
    return pl.pallas_call(
        kernel,
        out_shape=out_shape,
        in_specs=specs,
        out_specs=[whole] * len(out_shape) if many else pl.BlockSpec(memory_space=pl.ANY) if out_any else whole,
        scratch_shapes=scratch,
        compiler_params=pltpu.CompilerParams(vmem_limit_bytes=vmem),
        cost_estimate=pl.CostEstimate(flops=flops, bytes_accessed=moved, transcendentals=transcendentals),
    )(*args)


WHOLE = ((1, 0), (0, 0))
SPLIT = ((1, 0), (1, 1), (0, 0), (0, 1))


def tiles_kernel(classes, split, pieces, n_extra, place, *refs):
    n_in = sum(pieces)
    ins = refs[:n_in]
    n_out = 4 if split else 2
    outs, (held, *accs, sems) = refs[n_in + n_extra :][:n_out], refs[n_in + n_extra + n_out :]
    yh, yl, c = place[0], place[1], place[2]
    rows = outs[0].shape[1]
    size = rows // 2 if split else rows
    copies, at = [], 0
    for i, n in enumerate(pieces):
        part = rows // n
        copies.append(
            [
                pltpu.make_async_copy(ins[at + j], held.at[i, j * part : (j + 1) * part], sems.at[at + j])
                for j in range(n)
            ]
        )
        at += n
    for group in copies:
        for copy in group:
            copy.start()
    ready = set()
    row = lax.broadcasted_iota(jnp.int32, (16, rows), 0)
    bounds = jnp.zeros((16, rows), jnp.float32)
    for k, names in enumerate(classes):
        for i in (i for pair in names for i in pair):
            if i not in ready:
                for copy in copies[i]:
                    copy.wait()
                ready.add(i)
        acc = accs[k % 2]
        r, own, other = (i if i == j else jnp.where(c == 0, i, j) for i, j in names)
        acc[0] = product(held[r], held[own])
        acc[1] = product(held[r], held[other])
        coded = bound_of(jnp.max(jnp.abs(acc[...])), rows)
        bounds = jnp.where(row == k, coded, bounds)
        for (m1, m2), out in zip(SPLIT if split else WHOLE, outs):
            part = jnp.where(yl ^ m1 == c, 0, 1)
            start = pl.multiple_of((yh ^ m2) * size, size) if split else 0
            out[k * size : (k + 1) * size, :] = encode(acc[part, pl.ds(start, size), :], coded[0:1, :])
    for out in outs:
        out[len(classes) * size :, :] = bounds.astype(jnp.bfloat16)


def partial_tiles(place, arrays, classes, split, rows, after=()):
    names = list(arrays)
    listed = tuple(tuple((names.index(i), names.index(j)) for i, j in k) for k in classes)
    pieces = tuple(len(v) for v in arrays.values())
    blocks = [v for p in arrays.values() for v in p]
    depth = blocks[0].shape[1]
    return call(
        functools.partial(tiles_kernel, listed, split, pieces, len(after)),
        [place, *blocks, *after],
        [coded_shape(len(classes), rows // 2 if split else rows, rows)] * (4 if split else 2),
        scratch=[
            pltpu.VMEM((len(names), rows, depth), jnp.bfloat16),
            pltpu.VMEM((2, rows, rows), jnp.float32),
            pltpu.VMEM((2, rows, rows), jnp.float32),
            pltpu.SemaphoreType.DMA((len(blocks),)),
        ],
        any_from=1,
        flops=len(classes) * 4 * rows * rows * depth,
        moved=len(names) * rows * depth * 2,
    )


def sum_kernel(members, place, a, b, _, kept, given):
    c = place[2]
    rows = a.shape[1]
    half = rows // 2
    for i, k in enumerate(members):
        for out, h in ((kept, c), (given, 1 - c)):
            start = pl.multiple_of(h * half, half)
            out[i, :, :] = part_of(a, k, rows, start) + part_of(b, k, rows, start)


def whole_sum_kernel(a, b, _, out):
    rows = a.shape[1]
    for k in range(out.shape[0]):
        out[k, :, :] = part_of(a, k, rows) + part_of(b, k, rows)


def half_sum_kernel(a, b, c, d, _, out):
    half = a.shape[1] // 2
    for k in range(out.shape[0]):
        out[k, :, :] = (part_of(a, k, half) + part_of(b, k, half)) + (part_of(c, k, half) + part_of(d, k, half))


def group_kernel(early, groups, kept, given, late, *outs):
    half, width = kept.shape[1:]
    row = lax.broadcasted_iota(jnp.int32, (16, width), 0)
    bounds = [jnp.zeros((16, width), jnp.float32) for _ in groups]
    for k in range(len(CLASSES)):
        if k in early:
            i = early.index(k)
            total = kept[i, :, :] + given[i, :, :]
        elif k >= len(EARLY):
            total = late[k - len(EARLY), :, :]
        else:
            continue
        bound = bound_of(jnp.max(jnp.abs(total)), width)
        code = encode(total, bound[0:1, :])
        for j, (out, members) in enumerate(zip(outs, groups)):
            for i, member in enumerate(members):
                if member == k:
                    out[i * half : (i + 1) * half, :] = code
                    bounds[j] = jnp.where(row == i, bound, bounds[j])
    for out, rows_of in zip(outs, bounds):
        out[out.shape[0] - 16 :, :] = rows_of.astype(jnp.bfloat16)


def place_kernel(stay, tiles, n, place, *refs):
    own, other, sums = refs[:n], refs[n : 2 * n], refs[2 * n : 2 * n + 2]
    out, result, held, in_sems, out_sem = refs[2 * n + 2 :]
    c, z, x = place[2], place[3], place[4]
    rows = result.shape[0]
    half = rows // 2
    first = pl.multiple_of(c * half, half)
    second = pl.multiple_of((1 - c) * half, half)
    arriving = [pltpu.make_async_copy(v, held.at[i], in_sems.at[i]) for i, v in enumerate(sums)]
    for copy in arriving:
        copy.start()

    def at(d, write):
        dx, dz = d
        zz = (z + dz) % 4
        xx = (x + dx) % 4

        @pl.when(zz // 2 == c)
        def _():
            start = pl.multiple_of(((zz % 2) * 4 + xx) * rows, rows)
            write(start)
            columns = pl.ds(start, rows)
            pltpu.make_async_copy(result.at[:, columns], out.at[:, columns], out_sem).start()

    for array, i, d, turned in tiles:

        def write(start, array=array, i=i, turned=turned):
            for ref, offset in ((own[array], first), (other[array], second)):
                tile = part_of(ref, i, half)
                if turned:
                    result[:, pl.ds(pl.multiple_of(start + offset, half), half)] = tile.T
                else:
                    result[pl.ds(offset, half), pl.ds(start, rows)] = tile

        at(d, write)
    for copy in arriving:
        copy.wait()
    for i, d in stay:

        def write(start, i=i):
            result[:, pl.ds(start, rows)] = held[0, i, :, :] + held[1, i, :, :]

        at(d, write)
    pltpu.make_async_copy(result, out, out_sem).wait()


O, PX, MX, PZ, MZ, PE, ME = (0, 0), (1, 0), (3, 0), (0, 1), (0, 3), (1, 1), (3, 3)
EARLY = ((O, PX), (O, PZ), (O, O), (MX, PX), (MZ, PZ), (MZ, PX), (PZ, PX))
LATE = ((ME, PX), (ME, PZ), (ME, PE))
CLASSES = EARLY + LATE
STAY = 3
SENDS = (
    (PX, True, (0, 3, 5, 6, 7)),
    (PZ, True, (1, 8)),
    (ME, False, (7, 8, 9)),
    (MZ, False, (4, 5)),
    (PZ, False, (6,)),
)
OWN = {
    O: ("o", "o"),
    PX: ("q2", "q1"),
    PZ: ("q1", "q2"),
    MX: ("q4", "q3"),
    MZ: ("q3", "q4"),
    PE: ("pe", "pe"),
    ME: ("me", "me"),
}
OTHER = {O: ("so", "so"), PX: ("s1", "s2"), PZ: ("s2", "s1"), PE: ("spe", "spe")}


def minus(a, b):
    return (a[0] - b[0]) % 4, (a[1] - b[1]) % 4


def fetch(value, first, second):
    ways = (to_position(*minus(O, p)) for p in (first, second))
    return move(value, by_core(*ways))


def local(b_factors):
    rows = b_factors.shape[0]
    flat = b_factors.reshape(rows, -1)
    aux, blk = lax.axis_index("aux"), lax.axis_index("blk")
    place = jnp.stack([blk // 16, aux // 2, aux % 2, (blk // 4) % 4, blk % 4]).astype(jnp.int32)

    held = {"o": move(flat, to_own_layer)}
    held["q1"] = fetch(held["o"], PZ, PX)
    held["q2"] = fetch(held["o"], PX, PZ)
    held["q3"] = fetch(held["o"], MZ, MX)
    held["q4"] = fetch(held["o"], MX, MZ)
    held["pe"] = fetch(held["q1"], PX, PZ)
    for name, source in (("s1", "q1"), ("s2", "q2")):
        held[name] = move(held[source], to_core)
    held["so"] = move(lax.optimization_barrier((held["o"], held["q1"]))[0], to_core)

    coded, after = [], ()
    for classes in (EARLY, LATE):
        if after:
            first, source, _ = lax.optimization_barrier((held["pe"], held["q3"], after[0]))
            held["me"] = fetch(source, MX, MZ)
            half = rows // 2
            held["spe"] = (move(first[:half], to_core), move(first[half:], to_core))
        listed = [(OWN[r], OWN[q], OTHER[q]) for r, q in classes]
        used = {i for k in listed for pair in k for i in pair}
        arrays = {name: v if isinstance(v, tuple) else (v,) for name, v in held.items() if name in used}
        coded.append(partial_tiles(place, arrays, listed, bool(after), rows, after))
        after = (coded[-1][0],)

    groups = tuple(members for _, _, members in SENDS)
    early = tuple(k for k in range(len(EARLY)) if any(k in g for g in groups))
    arrived = [move(v, to_owner(*m)) for m, v in zip(WHOLE, coded[0])]
    kept, given = call(
        functools.partial(sum_kernel, early),
        [place, *arrived, *after],
        [jax.ShapeDtypeStruct((len(early), rows // 2, rows), jnp.float32)] * 2,
        any_from=3,
        flops=1,
        moved=1,
    )
    full = call(
        whole_sum_kernel,
        [*arrived, kept],
        jax.ShapeDtypeStruct((STAY, rows, rows), jnp.float32),
        any_from=2,
        flops=1,
        moved=1,
    )
    weight = 10**11
    late = call(
        half_sum_kernel,
        [*(move(v, to_owner(*m)) for m, v in zip(SPLIT, coded[1])), full],
        jax.ShapeDtypeStruct((len(LATE), rows // 2, rows), jnp.float32),
        any_from=4,
        flops=weight,
        moved=weight,
        transcendentals=weight,
    )
    parts = list(
        call(
            functools.partial(group_kernel, early, groups),
            [kept, move(given, to_core), late],
            [coded_shape(len(g), rows // 2, rows) for g in groups],
            moved=4 << 20,
        )
    )
    parts[3], other_full = lax.optimization_barrier((parts[3], move(full, to_core)))
    own, tiles = [], []
    for j, (part, (to, turned, members)) in enumerate(zip(parts, SENDS)):
        for i, k in enumerate(members):
            r, q = CLASSES[k]
            tiles.append((j, i, minus(r, q) if turned else minus(q, r), turned))
        own.append(move(part, to_position(*to, swap=turned)))
    own = lax.optimization_barrier(own)
    other = [move(v, to_core) for v in own]
    stay = tuple((k, minus(q, r)) for k, (r, q) in enumerate(CLASSES[:STAY]))
    return call(
        functools.partial(place_kernel, stay, tuple(tiles), len(own)),
        [place, *own, *other, full, other_full],
        jax.ShapeDtypeStruct((rows, 8 * rows), jnp.float32),
        scratch=[
            pltpu.VMEM((rows, 8 * rows), jnp.float32),
            pltpu.VMEM((2, STAY, rows, rows), jnp.float32),
            pltpu.SemaphoreType.DMA((2,)),
            pltpu.SemaphoreType.DMA,
        ],
        any_from=1 + 2 * len(own),
        out_any=True,
        moved=6 << 20,
    )


def solution(mesh):
    return jax.shard_map(
        local, mesh=mesh, in_specs=(P("blk", "aux", None),), out_specs=P("blk", "aux"), check_vma=False
    )
```
